512 devices in a mesh: row: 8 (over z), feat: 64 (over x, y, core).
Axes of the slice: x: 4, y: 8, z: 8, core: 2. Of those that a mesh axis runs over, the one named last changes fastest.
Arguments:
- logits: bfloat16 [32768, 1000], P(('row', 'feat')), may hold values from -200 to 200, as said below
- labels: int32 [32768], P(('row', 'feat')), may hold values from 0 to 999
- projection: bfloat16 [1000, 16], replicated, may hold values from -4 to 4
- bins: int32 [2048, 32768], P('feat', 'row'), may hold values from 0 to 63, as said below
- nbins: int32 [2048], P('feat'), may hold values from 2 to 64
- leaf: int32 [32768], P('row'), may hold values from 0 to 15
Outputs:
- relative_gain: float32 [16, 131072], P('row', 'feat')
The draws below stay inside these ranges and needn't reach their ends.
Inputs may be any that keep to these rules, and one draw needn't show every extreme that they name: `logits`: shows the class scores; some rows may lie far from zero. bins[f, i] < nbins[f].
All inputs are finite; a program needn't handle non-finite values.
Results may differ from the reference program's by a relative error of at most 0.0017.
Values may be sent and summed in bfloat16 or wider, within the bound.
A program may use at most 64 MiB of HBM per device.

```python
import math
import jax
import jax.numpy as jnp
from jax import lax

C = 1000
F = 2048
K = 16
BINS = 64
LEAVES = 16
ROWS = 32768
N_ROW = 8


def draw_logits(key, part):
    first = jax.random.fold_in(jax.random.fold_in(key, 3), 0)
    return (jax.random.normal(first, (ROWS, C), jnp.float32) * 3.0).astype(jnp.bfloat16)


def bin_counts(key):
    first, second = jax.random.split(jax.random.fold_in(key, 11))
    caps = jax.random.randint(first, (F // 32, 1), 4, BINS + 1)
    counts = jax.random.randint(second, (F // 32, 32), 2, BINS + 1)
    return jnp.minimum(counts, caps).reshape(F)


def draw_nbins(key, part):
    return bin_counts(key)


def draw_bins(key, part):
    counts = bin_counts(key)
    raw = jax.random.randint(jax.random.fold_in(key, 17), (F, ROWS), 0, 1 << 20)
    return raw % counts[:, None]


def place_ends(values, rng, least, high):
    spot = [jax.random.randint(jax.random.fold_in(rng, axis), (), 0, length) for axis, length in enumerate(values.shape)]
    longest = values.shape.index(max(values.shape))
    beside = spot[:longest] + [(spot[longest] + 1) % values.shape[longest]] + spot[longest + 1:]
    return values.at[tuple(spot)].set(least).at[tuple(beside)].set(high)


def normal_values(stream_key, dims, deviation, limit, kind=jnp.bfloat16):
    array = jax.random.normal(stream_key, dims, jnp.float32) * deviation
    return jnp.minimum(jnp.maximum(array, -limit), limit).astype(kind)


def setup_inputs(seed: int = 0) -> dict:
    key_of = jax.random.split(jax.random.key(seed), 7)
    logits = draw_logits(jax.random.fold_in(key_of[6], 71), 0)
    labels = place_ends(jax.random.randint(key_of[1], (ROWS,), 0, C), jax.random.fold_in(key_of[1], 1), 0, C - 1).astype(jnp.int32)
    projection = normal_values(key_of[2], (C, K), 1.0, 4.0)
    bins = draw_bins(jax.random.fold_in(key_of[6], 71), 0)
    nbins = draw_nbins(jax.random.fold_in(key_of[6], 71), 0)
    leaf = place_ends(jax.random.randint(key_of[5], (ROWS,), 0, LEAVES), jax.random.fold_in(key_of[5], 1), 0, LEAVES - 1).astype(jnp.int32)
    return dict(logits=logits, labels=labels, projection=projection, bins=bins, nbins=nbins, leaf=leaf)


ridge = 1.0
epsilon = 1e-6


def row_values(logits, labels, projection):
    scores = logits.astype(jnp.float32)
    highest = jnp.max(scores, axis=1, keepdims=True)
    expd = jnp.exp(scores - highest)
    probability = expd / jnp.sum(expd, axis=1, keepdims=True)
    classes = jnp.arange(logits.shape[1], dtype=jnp.int32)
    target = (labels[:, None] == classes[None, :]).astype(jnp.float32)
    gradient = (probability - target).astype(jnp.bfloat16)
    sketch = jnp.dot(gradient, projection, preferred_element_type=jnp.float32).astype(jnp.bfloat16)
    hessian = jnp.sum(probability * (1.0 - probability), axis=1).astype(jnp.bfloat16)
    return jnp.concatenate([sketch, hessian[:, None]], axis=1).astype(jnp.float32)


def shard_histogram(values, leaf_rows, bin_rows):
    rows = values.shape[0]
    width = math.gcd(F, 256)
    groups = F // width
    columns = values.shape[1]
    grouped = bin_rows.reshape(rows, groups, width).transpose(1, 0, 2)
    offsets = jnp.arange(width, dtype=jnp.int32)
    spread = jnp.broadcast_to(values[:, None, :], (rows, width, columns)).reshape(rows * width, columns)

    def one_group(group_bins):
        segment = ((offsets[None, :] * BINS + group_bins) * LEAVES + leaf_rows[:, None]).reshape(-1)
        summed = jax.ops.segment_sum(spread, segment.astype(jnp.int32), num_segments=width * BINS * LEAVES)
        return summed.reshape(width, BINS, LEAVES, columns)

    stacked = lax.map(one_group, grouped)
    return stacked.reshape(F, BINS, LEAVES, columns)


def split_gains(histogram, nbins):
    left = jnp.cumsum(histogram, axis=3)
    total = left[..., -1:]
    right = total - left

    def score(sums):
        return jnp.sum(sums[:, :-1] * sums[:, :-1] / (sums[:, -1:] + ridge), axis=1)

    gain = score(left) + score(right) - score(total)
    valid = jnp.arange(histogram.shape[3], dtype=jnp.int32)[None, :] < (nbins[:, None] - 1)
    return jnp.where(valid[None], gain, jnp.zeros_like(gain))


def reference(logits, labels, projection, bins, nbins, leaf):
    values = row_values(logits, labels, projection)
    shard_rows = ROWS // N_ROW
    total = jnp.zeros((F, BINS, LEAVES, K + 1), jnp.float32)
    for shard in range(N_ROW):
        low = shard * shard_rows
        part = shard_histogram(values[low:low + shard_rows], leaf[low:low + shard_rows], bins[:, low:low + shard_rows].T)
        total = total + part
    histogram = total.transpose(2, 3, 0, 1)
    gain = split_gains(histogram, nbins)
    best = jnp.max(gain, axis=(1, 2))
    relative = gain / (best[:, None, None] + epsilon)
    return relative.reshape(LEAVES, F * BINS)
```

```python
import functools

import jax
import jax.numpy as jnp
from jax import lax
from jax.experimental import pallas as pl
from jax.experimental.pallas import tpu as pltpu
from jax.sharding import PartitionSpec as P

BINS = 64
LEAVES = 16
K = 16
GROUP = 4
LANES = 128
MESH = pl.DeviceIdType.MESH
NT = (((1,), (1,)), ((), ()))

ridge = 1.0
epsilon = 1e-6


def near_first(t):
    return ((t + 1) // 2) * (2 * (t % 2) - 1)


def kernel(
    NX,
    NY,
    NZ,
    logits_any,
    labels_ref,
    proj_ref,
    bins_any,
    nbins_ref,
    leaf_ref,
    out_ref,
    logits_v,
    bins_v,
    grad,
    bins_s,
    leaf_s,
    zsk_s,
    zhs_s,
    bins_r,
    leaf_r,
    zsk_r,
    zhs_r,
    bins_f,
    leaf_f,
    sk,
    hs,
    weights,
    onehot,
    acc,
    hist_r,
    sums,
    gain_s,
    gain_r,
    max1_s,
    max1_r,
    max2_s,
    max2_r,
    max3_s,
    max3_r,
    local_sem,
    zs_sem,
    zr_sem,
    ys_sem,
    yr_sem,
    xs_sem,
    xr_sem,
    hist_sem,
    gs_sem,
    gr_sem,
    m1s_sem,
    m1r_sem,
    m2s_sem,
    m2r_sem,
    m3s_sem,
    m3r_sem,
):
    HZ = NZ // 2
    LP = LEAVES // NZ
    rows = labels_ref.shape[1]
    z = lax.axis_index("row")
    feat = lax.axis_index("feat")
    c = feat % 2
    y = (feat // 2) % NY
    x = feat // (2 * NY)
    h = z // HZ
    slot = (z % HZ) * 2 + c

    def dev(x_, y_, z_, c_):
        return (z_, (x_ * NY + y_) * 2 + c_)

    def remote(src, dst, send, recv, device):
        return pltpu.make_async_remote_copy(
            src_ref=src, dst_ref=dst, send_sem=send, recv_sem=recv, device_id=device, device_id_type=MESH
        )

    cp_logits = pltpu.make_async_copy(logits_any, logits_v, local_sem.at[0])
    cp_bins = pltpu.make_async_copy(bins_any, bins_v, local_sem.at[1])
    cp_logits.start()
    cp_bins.start()

    barrier = pltpu.get_barrier_semaphore()

    def greet(device):
        pl.semaphore_signal(barrier, inc=1, device_id=device, device_id_type=MESH)

    @pl.loop(1, 2 * NZ)
    def _(i):
        other = (z * 2 + c + i) % (2 * NZ)
        greet(dev(x, y, other // 2, other % 2))

    @pl.loop(1, NY)
    def _(i):
        greet(dev(x, (y + i) % NY, z, c))

    @pl.loop(1, NX)
    def _(i):
        greet(dev((x + i) % NX, y, z, c))
        greet(dev((x + i) % NX, y, z, 1 - c))

    with jax.named_scope("softmax"):
        cp_logits.wait()
        lane = lax.broadcasted_iota(jnp.int32, (rows, rows), 1)
        line = lax.broadcasted_iota(jnp.int32, (rows, rows), 0)
        spread = jnp.where(lane == line, labels_ref[...].astype(jnp.float32), 0.0)
        target = jnp.sum(spread, axis=1, keepdims=True).astype(jnp.int32)
        scores = logits_v[...].astype(jnp.float32)
        highest = jnp.max(scores, axis=1, keepdims=True)
        expd = jnp.exp(scores - highest)
        probability = expd * (1.0 / jnp.sum(expd, axis=1, keepdims=True))
        classes = lax.broadcasted_iota(jnp.int32, scores.shape, 1)
        gradient = probability - jnp.where(classes == target, 1.0, 0.0)
        grad[...] = jnp.zeros_like(grad)
        grad[pl.ds(pl.multiple_of(c * rows, rows), rows), :] = gradient.astype(jnp.bfloat16)
        sketch = lax.dot_general(proj_ref[...], grad[...], NT, preferred_element_type=jnp.float32)
        zsk_s[...] = sketch.astype(jnp.bfloat16)
        hessian = jnp.sum(probability * (1.0 - probability), axis=1, keepdims=True)
        hessian = hessian.astype(jnp.bfloat16).astype(jnp.float32)
        lane = lax.broadcasted_iota(jnp.int32, (rows, LANES), 1)
        line = lax.broadcasted_iota(jnp.int32, (rows, LANES), 0)
        zhs_s[...] = jnp.sum(jnp.where(lane == line + c * rows, hessian, 0.0), axis=0, keepdims=True)

    with jax.named_scope("barrier"):
        pl.semaphore_wait(barrier, 2 * NZ - 1 + NY - 1 + 2 * (NX - 1))

    def to_column(i, src, dst, kind, act):
        device = dev(x, y, (z + i) % NZ, h)
        send, recv = zs_sem.at[kind, i], zr_sem.at[kind, slot]
        here = (i == 0) & (c == h)

        @pl.when(here)
        def _():
            if act == "start":
                pltpu.make_async_copy(src, dst, recv).start()

        @pl.when(jnp.logical_not(here))
        def _():
            copy = remote(src, dst, send, recv, device)
            if act == "start":
                copy.start()
            else:
                copy.wait_send()

    def column_values(i, act):
        to_column(i, zsk_s, zsk_r.at[slot], 0, act)
        to_column(i, zhs_s, zhs_r.at[slot], 1, act)

    def column_bins(i, act):
        to_column(i, bins_s.at[(z + i) % NZ], bins_r.at[slot], 2, act)
        to_column(i, leaf_s, leaf_r.at[slot], 3, act)

    @pl.loop(0, NZ)
    def _(i):
        column_values(i, "start")

    with jax.named_scope("regroup"):
        cp_bins.wait()
        width = NY * LANES
        for d in range(NZ):
            four = bins_v[d * GROUP : (d + 1) * GROUP, :].astype(jnp.float32)
            bins_s[d] = jnp.concatenate(
                [four[:, i * width : (i + 1) * width] for i in range(NX)], axis=0
            ).astype(jnp.bfloat16)
        half = NX * NY // 2
        leaf_s[...] = leaf_ref[pl.ds(pl.multiple_of(c * half, half), half), :].astype(jnp.float32).astype(jnp.bfloat16)

    @pl.loop(0, NZ)
    def _(i):
        column_bins(i, "start")

    def block_copies(step, xs, ys, device, send, recv):
        return (
            remote(sk.at[xs, ys], sk.at[xs, ys], send.at[0, step], recv.at[0], device),
            remote(hs.at[xs, ys], hs.at[xs, ys], send.at[1, step], recv.at[1], device),
        )

    with jax.named_scope("zvalues"):
        lane = lax.broadcasted_iota(jnp.int32, (1, LANES), 1)
        first = lane < rows

        @pl.loop(0, 2 * HZ)
        def _(i):
            remote(zsk_s, zsk_r.at[i], zs_sem.at[0, 0], zr_sem.at[0, i], dev(x, y, z, c)).wait_recv()
            remote(zhs_s, zhs_r.at[i], zs_sem.at[0, 0], zr_sem.at[1, i], dev(x, y, z, c)).wait_recv()

        for i in range(HZ):
            span = slice(i * LANES, (i + 1) * LANES)
            sk[x, y, :, span] = jnp.where(
                first, zsk_r[2 * i].astype(jnp.float32), zsk_r[2 * i + 1].astype(jnp.float32)
            ).astype(jnp.bfloat16)
            hs[x, y, :, span] = jnp.where(first, zhs_r[2 * i], zhs_r[2 * i + 1])

    def y_copies(t):
        return block_copies(
            t, x, y, dev(x, (y + near_first(t) + NY) % NY, z, c), ys_sem, yr_sem.at[y]
        )

    def x_copies(i, ys):
        return block_copies(
            ys, x, ys, dev((x + i) % NX, y, z, c), xs_sem.at[i], xr_sem.at[x, ys]
        )

    @pl.loop(1, NY)
    def _(t):
        for copy in y_copies(t):
            copy.start()

    acc[...] = jnp.zeros_like(acc)

    with jax.named_scope("zbins"):
        for i in range(2 * HZ):
            remote(bins_s.at[0], bins_r.at[i], zs_sem.at[0, 0], zr_sem.at[2, i], dev(x, y, z, c)).wait_recv()
            remote(leaf_s, leaf_r.at[i], zs_sem.at[0, 0], zr_sem.at[3, i], dev(x, y, z, c)).wait_recv()
            for j in range(NY):
                bins_f[i, j] = bins_r[i, :, j * LANES : (j + 1) * LANES].astype(jnp.float32)
            leaf_f[i // 2, (i % 2) * half : (i % 2 + 1) * half] = leaf_r[i].astype(jnp.float32)

    bin_ids = lax.broadcasted_iota(jnp.int32, (BINS, LANES), 0).astype(jnp.float32).astype(jnp.bfloat16)
    leaf_ids = lax.broadcasted_iota(jnp.int32, (LEAVES, LANES), 0).astype(jnp.float32).astype(jnp.bfloat16)
    one, nil = jnp.bfloat16(1), jnp.bfloat16(0)

    def add_block(xs, ys):
        for i in range(HZ):
            span = slice(i * LANES, (i + 1) * LANES)
            leaf = leaf_f[i, pl.ds(xs * NY + ys, 1), :]
            leaf = jnp.broadcast_to(leaf, (LEAVES, LANES)).astype(jnp.bfloat16)
            tile = sk[xs, ys, :, span]
            for l in range(LEAVES):
                weights[l * K : (l + 1) * K, span] = jnp.where(leaf == jnp.bfloat16(l), tile, nil)
            hess = jnp.broadcast_to(hs[xs, ys, :, span], (LEAVES, LANES)).astype(jnp.bfloat16)
            weights[LEAVES * K :, span] = jnp.where(leaf == leaf_ids, hess, nil)
            for side in range(2):
                for f in range(GROUP):
                    ids = bins_f[2 * i + side, ys, pl.ds(xs * GROUP + f, 1), :]
                    ids = jnp.broadcast_to(ids, (BINS, LANES)).astype(jnp.bfloat16)
                    onehot[side, f * BINS : (f + 1) * BINS, span] = jnp.where(ids == bin_ids, one, nil)
        for side in range(2):
            acc[side] += lax.dot_general(weights[...], onehot[side], NT, preferred_element_type=jnp.float32)

    def forward(ys):
        @pl.loop(1, NX)
        def _(i):
            for copy in x_copies(i, ys):
                copy.start()

    with jax.named_scope("ownslab"):

        @pl.loop(0, NY)
        def _(t):
            ys = (y + near_first(t) + NY) % NY

            @pl.when(t > 0)
            def _():
                for copy in block_copies(t, x, ys, dev(x, y, z, c), ys_sem, yr_sem.at[ys]):
                    copy.wait_recv()

            forward(ys)
            add_block(x, ys)

    with jax.named_scope("slabs"):

        @pl.loop(0, NY * (NX - 1))
        def _(t):
            ys = (y + near_first(t // (NX - 1)) + NY) % NY
            xs = (x + near_first(t % (NX - 1) + 1) + NX) % NX
            for copy in block_copies(ys, xs, ys, dev(x, y, z, c), xs_sem.at[1], xr_sem.at[xs, ys]):
                copy.wait_recv()
            add_block(xs, ys)

    with jax.named_scope("cores"):
        swap = remote(acc.at[1 - c], hist_r, hist_sem.at[0], hist_sem.at[1], dev(x, y, z, 1 - c))
        swap.start()
        swap.wait_recv()

    with jax.named_scope("gains"):
        hist = acc[c] + hist_r[...]
        cols = GROUP * BINS
        src = lax.broadcasted_iota(jnp.int32, (cols, cols), 0)
        dst = lax.broadcasted_iota(jnp.int32, (cols, cols), 1)
        same = (src // BINS) == (dst // BINS)
        upto = jnp.where(same & (src <= dst), 1.0, 0.0).astype(jnp.bfloat16)
        past = jnp.where(same & (src > dst), 1.0, 0.0).astype(jnp.bfloat16)
        left = jnp.zeros_like(hist)
        right = jnp.zeros_like(hist)
        rest = hist
        for _ in range(3):
            piece = rest.astype(jnp.bfloat16)
            rest = rest - piece.astype(jnp.float32)
            left += jnp.dot(piece, upto, preferred_element_type=jnp.float32)
            right += jnp.dot(piece, past, preferred_element_type=jnp.float32)
        for i in range(cols // LANES):
            sums[0, i] = left[:, i * LANES : (i + 1) * LANES]
            sums[1, i] = right[:, i * LANES : (i + 1) * LANES]

        def side_sums(side, lines):
            return jnp.concatenate([sums[side, i, lines, :] for i in range(cols // LANES)], axis=1)

        def squares(get):
            total = jnp.zeros((LEAVES, cols), jnp.float32)
            for k in range(K):
                s = get(pl.ds(k, LEAVES, stride=K))
                total += s * s
            return total / (get(slice(LEAVES * K, LEAVES * K + LEAVES)) + ridge)

        gain = (
            squares(lambda r: side_sums(0, r))
            + squares(lambda r: side_sums(1, r))
            - squares(lambda r: side_sums(0, r) + side_sums(1, r))
        )
        lane = lax.broadcasted_iota(jnp.int32, (1, cols), 1)
        counts = jnp.zeros((1, cols), jnp.int32)
        for f in range(GROUP):
            counts = jnp.where(lane // BINS == f, nbins_ref[z * GROUP + f], counts)
        gain = jnp.where(lane % BINS < counts - 1, gain, 0.0)
        for i in range(NZ):
            gain_s[i] = gain[i * LP : (i + 1) * LP]
        best = jnp.max(gain, axis=1, keepdims=True)
        max1_s[...] = jnp.broadcast_to(best, (LEAVES, LANES))

    def gain_copy(i):
        other = (z + i) % NZ
        return remote(gain_s.at[other], gain_r.at[z], gs_sem.at[i], gr_sem.at[z], dev(x, y, other, c))

    def max1_copy(i):
        return remote(max1_s, max1_r.at[y], m1s_sem.at[i], m1r_sem.at[y], dev(x, (y + i) % NY, z, c))

    mine = x * 2 + c

    def max2_copy(i):
        other = (mine + i) % (2 * NX)
        return remote(max2_s, max2_r.at[mine], m2s_sem.at[i], m2r_sem.at[mine], dev(other // 2, y, z, other % 2))

    def max3_copy(i):
        other = (z + i) % NZ
        return remote(max3_s.at[other], max3_r.at[z], m3s_sem.at[i], m3r_sem.at[z], dev(x, y, other, c))

    with jax.named_scope("max1"):

        @pl.loop(1, NY)
        def _(i):
            max1_copy(i).start()

        @pl.loop(1, NZ)
        def _(i):
            gain_copy(i).start()

        best = max1_s[...]
        max1_r[y] = best

        @pl.loop(1, NY)
        def _(i):
            other = (y + i) % NY
            remote(max1_s, max1_r.at[other], m1s_sem.at[0], m1r_sem.at[other], dev(x, y, z, c)).wait_recv()

        max2_s[...] = functools.reduce(jnp.maximum, [max1_r[i] for i in range(NY)])

    with jax.named_scope("max2"):

        @pl.loop(1, 2 * NX)
        def _(i):
            max2_copy(i).start()

        max2_r[mine] = max2_s[...]

        @pl.loop(1, 2 * NX)
        def _(i):
            other = (mine + i) % (2 * NX)
            remote(max2_s, max2_r.at[other], m2s_sem.at[0], m2r_sem.at[other], dev(x, y, z, c)).wait_recv()

        best = functools.reduce(jnp.maximum, [max2_r[i] for i in range(2 * NX)])
        for i in range(NZ):
            max3_s[i] = best[i * LP : (i + 1) * LP]

    with jax.named_scope("max3"):

        @pl.loop(1, NZ)
        def _(i):
            max3_copy(i).start()

        max3_r[z] = max3_s[z]
        gain_r[z] = gain_s[z]

        @pl.loop(1, NZ)
        def _(i):
            other = (z + i) % NZ
            remote(gain_s.at[0], gain_r.at[other], gs_sem.at[0], gr_sem.at[other], dev(x, y, z, c)).wait_recv()
            remote(max3_s.at[0], max3_r.at[other], m3s_sem.at[0], m3r_sem.at[other], dev(x, y, z, c)).wait_recv()

        best = functools.reduce(jnp.maximum, [max3_r[i] for i in range(NZ)])[:, :1]
        for i in range(NZ):
            out_ref[:, i * cols : (i + 1) * cols] = gain_r[i] / (best + epsilon)

    with jax.named_scope("sends"):

        @pl.loop(0, NZ)
        def _(i):
            column_values(i, "wait")
            column_bins(i, "wait")

        @pl.loop(1, NY)
        def _(t):
            for copy in y_copies(t):
                copy.wait_send()

        @pl.loop(0, NY)
        def _(t):
            @pl.loop(1, NX)
            def _(i):
                for copy in x_copies(i, t):
                    copy.wait_send()

        swap.wait_send()

        @pl.loop(1, NZ)
        def _(i):
            gain_copy(i).wait_send()
            max3_copy(i).wait_send()

        @pl.loop(1, NY)
        def _(i):
            max1_copy(i).wait_send()

        @pl.loop(1, 2 * NX)
        def _(i):
            max2_copy(i).wait_send()


def on_device(NX, NY, NZ, logits, labels, projection, bins, nbins, leaf):
    bf16, f32 = jnp.bfloat16, jnp.float32
    HZ = NZ // 2
    LP = LEAVES // NZ
    rows, classes = logits.shape
    span = HZ * LANES
    cols = GROUP * BINS
    tall = LEAVES * (K + 1)
    VMEM, DMA = pltpu.VMEM, pltpu.SemaphoreType.DMA
    vmem = pl.BlockSpec(memory_space=pltpu.VMEM)
    smem = pl.BlockSpec(memory_space=pltpu.SMEM)
    hbm = pl.BlockSpec(memory_space=pl.ANY)
    half = NX * NY // 2
    bin_block = (GROUP * NX, NY * LANES)
    return pl.pallas_call(
        functools.partial(kernel, NX, NY, NZ),
        out_shape=jax.ShapeDtypeStruct((LP, NZ * cols), f32),
        in_specs=[hbm, vmem, vmem, hbm, smem, vmem],
        out_specs=vmem,
        scratch_shapes=[
            VMEM(logits.shape, bf16),
            VMEM(bins.shape, jnp.int32),
            VMEM((2 * rows, classes), bf16),
            VMEM((NZ, *bin_block), bf16),
            VMEM((half, LANES), bf16),
            VMEM((K, LANES), bf16),
            VMEM((1, LANES), f32),
            VMEM((NZ, *bin_block), bf16),
            VMEM((NZ, half, LANES), bf16),
            VMEM((NZ, K, LANES), bf16),
            VMEM((NZ, 1, LANES), f32),
            VMEM((NZ, NY, GROUP * NX, LANES), f32),
            VMEM((HZ, 2 * half, LANES), f32),
            VMEM((NX, NY, K, span), bf16),
            VMEM((NX, NY, 1, span), f32),
            VMEM((tall, span), bf16),
            VMEM((2, cols, span), bf16),
            VMEM((2, tall, cols), f32),
            VMEM((tall, cols), f32),
            VMEM((2, cols // LANES, tall, LANES), f32),
            VMEM((NZ, LP, cols), f32),
            VMEM((NZ, LP, cols), f32),
            VMEM((LEAVES, LANES), f32),
            VMEM((NY, LEAVES, LANES), f32),
            VMEM((LEAVES, LANES), f32),
            VMEM((2 * NX, LEAVES, LANES), f32),
            VMEM((NZ, LP, LANES), f32),
            VMEM((NZ, LP, LANES), f32),
            DMA((2,)),
            DMA((4, NZ)),
            DMA((4, NZ)),
            DMA((2, NY)),
            DMA((NY, 2)),
            DMA((NX, 2, NY)),
            DMA((NX, NY, 2)),
            DMA((2,)),
            DMA((NZ,)),
            DMA((NZ,)),
            DMA((NY,)),
            DMA((NY,)),
            DMA((2 * NX,)),
            DMA((2 * NX,)),
            DMA((NZ,)),
            DMA((NZ,)),
        ],
        compiler_params=pltpu.CompilerParams(
            collective_id=0, has_side_effects=True, vmem_limit_bytes=40 * 2**20
        ),
        cost_estimate=pl.CostEstimate(
            flops=2 * tall * 2 * cols * NX * NY * span, bytes_accessed=2**20, transcendentals=rows * classes
        ),
    )(
        logits,
        labels.reshape(1, rows),
        projection.T,
        bins,
        nbins,
        leaf.reshape(2 * half, LANES),
    )


def solution(mesh, NX=4, NY=8):
    return jax.shard_map(
        functools.partial(on_device, NX, NY, mesh.shape["row"]),
        mesh=mesh,
        in_specs=(
            P(("row", "feat"), None),
            P(("row", "feat")),
            P(),
            P("feat", "row"),
            P("feat"),
            P("row"),
        ),
        out_specs=P("row", "feat"),
        check_vma=False,
    )
```

```python
import functools

import jax
import jax.numpy as jnp
from jax import lax
from jax.experimental import pallas as pl
from jax.experimental.pallas import tpu as pltpu
from jax.sharding import PartitionSpec as P

BINS = 64
LEAVES = 16
K = 16
GROUP = 4
QUAD = 4
LANES = 128
MESH = pl.DeviceIdType.MESH
NT = (((1,), (1,)), ((), ()))

ridge = 1.0
epsilon = 1e-6


def near_first(t):
    return ((t + 1) // 2) * (2 * (t % 2) - 1)


def far_first(t, n):
    return n // 2 + near_first(t)


def kernel(
    NX,
    NY,
    NZ,
    logits_any,
    labels_any,
    proj_any,
    bins_any,
    nbins_any,
    leaf_any,
    out_ref,
    logits_v,
    labels_ref,
    proj_ref,
    bins_v,
    nbins_ref,
    leaf_ref,
    grad,
    bins_s,
    leaf_s,
    zsk_s,
    zhs_s,
    bins_r,
    leaf_r,
    zsk_r,
    zhs_r,
    bins_f,
    leaf_f,
    sk,
    hs,
    weights,
    onehot,
    acc,
    hist_r,
    sums,
    gain_s,
    gain_r,
    pair_s,
    pair_r,
    best_s,
    best_r,
    local_sem,
    zs_sem,
    zr_sem,
    ys_sem,
    yr_sem,
    xs_sem,
    xr_sem,
    hist_sem,
    gs_sem,
    gr_sem,
    pair_sem,
    bs_sem,
    br_sem,
):
    HZ = NZ // 2
    LP = LEAVES // NZ
    rows = labels_ref.shape[1]
    z = lax.axis_index("row")
    feat = lax.axis_index("feat")
    c = feat % 2
    y = (feat // 2) % NY
    x = feat // (2 * NY)
    h = z // HZ
    slot = (z % HZ) * 2 + c

    def dev(x_, y_, z_, c_):
        return (z_, (x_ * NY + y_) * 2 + c_)

    def remote(src, dst, send, recv, device):
        return pltpu.make_async_remote_copy(
            src_ref=src, dst_ref=dst, send_sem=send, recv_sem=recv, device_id=device, device_id_type=MESH
        )

    operands = (
        (bins_any, bins_v),
        (logits_any, logits_v),
        (labels_any, labels_ref),
        (proj_any, proj_ref),
        (leaf_any, leaf_ref),
        (nbins_any, nbins_ref),
    )
    fetches = [pltpu.make_async_copy(src, dst, local_sem.at[i]) for i, (src, dst) in enumerate(operands)]
    for fetch in fetches:
        fetch.start()

    barrier = pltpu.get_barrier_semaphore()

    def greet(device):
        pl.semaphore_signal(barrier, inc=1, device_id=device, device_id_type=MESH)

    @pl.loop(1, 2 * NZ)
    def _(i):
        other = (z * 2 + c + i) % (2 * NZ)
        greet(dev(x, y, other // 2, other % 2))

    @pl.loop(1, NY)
    def _(i):
        greet(dev(x, (y + i) % NY, z, c))

    @pl.loop(1, NX)
    def _(i):
        greet(dev((x + i) % NX, y, z, c))

    with jax.named_scope("softmax"):
        for fetch in fetches[1:4]:
            fetch.wait()
        lane = lax.broadcasted_iota(jnp.int32, (rows, rows), 1)
        line = lax.broadcasted_iota(jnp.int32, (rows, rows), 0)
        spread = jnp.where(lane == line, labels_ref[...].astype(jnp.float32), 0.0)
        target = jnp.sum(spread, axis=1, keepdims=True).astype(jnp.int32)
        scores = logits_v[...].astype(jnp.float32)
        highest = jnp.max(scores, axis=1, keepdims=True)
        expd = jnp.exp(scores - highest)
        probability = expd * (1.0 / jnp.sum(expd, axis=1, keepdims=True))
        classes = lax.broadcasted_iota(jnp.int32, scores.shape, 1)
        gradient = probability - jnp.where(classes == target, 1.0, 0.0)
        grad[...] = jnp.zeros_like(grad)
        grad[pl.ds(pl.multiple_of(c * rows, rows), rows), :] = gradient.astype(jnp.bfloat16)
        sketch = lax.dot_general(proj_ref[...], grad[...], NT, preferred_element_type=jnp.float32)
        zsk_s[...] = sketch.astype(jnp.bfloat16)
        hessian = jnp.sum(probability * (1.0 - probability), axis=1, keepdims=True)
        hessian = hessian.astype(jnp.bfloat16).astype(jnp.float32)
        lane = lax.broadcasted_iota(jnp.int32, (rows, LANES), 1)
        line = lax.broadcasted_iota(jnp.int32, (rows, LANES), 0)
        zhs_s[...] = jnp.sum(jnp.where(lane == line + c * rows, hessian, 0.0), axis=0, keepdims=True)

    with jax.named_scope("barrier"):
        pl.semaphore_wait(barrier, 2 * NZ - 1 + NY - 1 + NX - 1)

    def to_column(t, src, dst, kind, act):
        device = dev(x, y, (z + far_first(t, NZ)) % NZ, h)
        send, recv = zs_sem.at[kind, t], zr_sem.at[kind, slot]
        here = (t == NZ - 1) & (c == h)

        @pl.when(here)
        def _():
            if act == "start":
                pltpu.make_async_copy(src, dst, recv).start()

        @pl.when(jnp.logical_not(here))
        def _():
            copy = remote(src, dst, send, recv, device)
            if act == "start":
                copy.start()
            else:
                copy.wait_send()

    def column_values(i, act):
        to_column(i, zsk_s, zsk_r.at[slot], 0, act)
        to_column(i, zhs_s, zhs_r.at[slot], 1, act)

    def column_bins(i, act):
        to_column(i, bins_s.at[(z + far_first(i, NZ)) % NZ], bins_r.at[slot], 2, act)
        to_column(i, leaf_s, leaf_r.at[slot], 3, act)

    @pl.loop(0, NZ)
    def _(i):
        column_values(i, "start")

    with jax.named_scope("regroup"):
        fetches[0].wait()
        fetches[4].wait()
        width = NY * LANES
        for d in range(NZ):
            four = bins_v[d * GROUP : (d + 1) * GROUP, :].astype(jnp.float32)
            bins_s[d] = jnp.concatenate(
                [four[:, i * width : (i + 1) * width] for i in range(NX)], axis=0
            ).astype(jnp.bfloat16)
        half = NX * NY // 2
        leaf_s[...] = leaf_ref[pl.ds(pl.multiple_of(c * half, half), half), :].astype(jnp.float32).astype(jnp.bfloat16)

    @pl.loop(0, NZ)
    def _(i):
        column_bins(i, "start")

    def block_copies(step, xs, ys, device, send, recv):
        return (
            remote(sk.at[xs, ys], sk.at[xs, ys], send.at[0, step], recv.at[0], device),
            remote(hs.at[xs, ys], hs.at[xs, ys], send.at[1, step], recv.at[1], device),
        )

    with jax.named_scope("zvalues"):
        lane = lax.broadcasted_iota(jnp.int32, (1, LANES), 1)
        first = lane < rows

        @pl.loop(0, 2 * HZ)
        def _(i):
            remote(zsk_s, zsk_r.at[i], zs_sem.at[0, 0], zr_sem.at[0, i], dev(x, y, z, c)).wait_recv()
            remote(zhs_s, zhs_r.at[i], zs_sem.at[0, 0], zr_sem.at[1, i], dev(x, y, z, c)).wait_recv()

        for i in range(HZ):
            span = slice(i * LANES, (i + 1) * LANES)
            sk[x, y, :, span] = jnp.where(
                first, zsk_r[2 * i].astype(jnp.float32), zsk_r[2 * i + 1].astype(jnp.float32)
            ).astype(jnp.bfloat16)
            hs[x, y, :, span] = jnp.where(first, zhs_r[2 * i], zhs_r[2 * i + 1])

    def y_copies(t):
        device = dev(x, (y + far_first(t, NY)) % NY, z, c)
        return block_copies(t, x, y, device, ys_sem, yr_sem.at[y])

    def x_copies(t, ys):
        device = dev((x + far_first(t, NX)) % NX, y, z, c)
        return block_copies(ys, x, ys, device, xs_sem.at[t], xr_sem.at[x, ys])

    def forward(ys):
        @pl.loop(0, NX - 1)
        def _(t):
            for copy in x_copies(t, ys):
                copy.start()

    @pl.loop(0, NY - 1)
    def _(t):
        for copy in y_copies(t):
            copy.start()

    forward(y)
    acc[...] = jnp.zeros_like(acc)

    def near_y(t):
        return (y + near_first(t) + NY) % NY

    def await_y(t):
        ys = near_y(t)
        for copy in block_copies(0, x, ys, dev(x, y, z, c), ys_sem, yr_sem.at[ys]):
            copy.wait_recv()
        forward(ys)

    pl.loop(1, QUAD)(await_y)

    with jax.named_scope("zbins"):
        for i in range(2 * HZ):
            remote(bins_s.at[0], bins_r.at[i], zs_sem.at[0, 0], zr_sem.at[2, i], dev(x, y, z, c)).wait_recv()
            remote(leaf_s, leaf_r.at[i], zs_sem.at[0, 0], zr_sem.at[3, i], dev(x, y, z, c)).wait_recv()
            for j in range(NY):
                bins_f[i, j] = bins_r[i, :, j * LANES : (j + 1) * LANES].astype(jnp.float32)
            leaf_f[i // 2, (i % 2) * half : (i % 2 + 1) * half] = leaf_r[i].astype(jnp.float32)

    bin_ids = lax.broadcasted_iota(jnp.int32, (BINS, LANES), 0).astype(jnp.float32).astype(jnp.bfloat16)
    leaf_ids = lax.broadcasted_iota(jnp.int32, (LEAVES, LANES), 0).astype(jnp.float32).astype(jnp.bfloat16)
    one, nil = jnp.bfloat16(1), jnp.bfloat16(0)

    def build(xs, quad):
        for b in range(QUAD):
            ys = near_y(quad * QUAD + b)
            for i in range(HZ):
                src = slice(i * LANES, (i + 1) * LANES)
                dst = slice((b * HZ + i) * LANES, (b * HZ + i + 1) * LANES)
                leaf = leaf_f[i, pl.ds(xs * NY + ys, 1), :]
                leaf = jnp.broadcast_to(leaf, (LEAVES, LANES)).astype(jnp.bfloat16)
                tile = sk[xs, ys, :, src]
                for l in range(LEAVES):
                    weights[l * K : (l + 1) * K, dst] = jnp.where(leaf == jnp.bfloat16(l), tile, nil)
                hess = jnp.broadcast_to(hs[xs, ys, :, src], (LEAVES, LANES)).astype(jnp.bfloat16)
                weights[LEAVES * K :, dst] = jnp.where(leaf == leaf_ids, hess, nil)
                for side in range(2):
                    for f in range(GROUP):
                        ids = bins_f[2 * i + side, ys, pl.ds(xs * GROUP + f, 1), :]
                        ids = jnp.broadcast_to(ids, (BINS, LANES)).astype(jnp.bfloat16)
                        onehot[side, f * BINS : (f + 1) * BINS, dst] = jnp.where(ids == bin_ids, one, nil)

    def add_side(side):
        acc[side] += lax.dot_general(weights[...], onehot[side], NT, preferred_element_type=jnp.float32)

    def add_quad(xs, quad):
        build(xs, quad)
        add_side(0)
        add_side(1)

    with jax.named_scope("ownslab"):

        @pl.loop(0, NY // QUAD)
        def _(quad):
            @pl.when(quad > 0)
            def _():
                pl.loop(quad * QUAD, (quad + 1) * QUAD)(await_y)

            add_quad(x, quad)

    def await_x(t):
        quad, xs = t // (NX - 1), (x + near_first(t % (NX - 1) + 1) + NX) % NX

        @pl.loop(quad * QUAD, (quad + 1) * QUAD)
        def _(i):
            ys = near_y(i)
            for copy in block_copies(0, xs, ys, dev(x, y, z, c), xs_sem.at[0], xr_sem.at[xs, ys]):
                copy.wait_recv()

        return xs, quad

    swap = remote(acc.at[1 - c], hist_r, hist_sem.at[0], hist_sem.at[1], dev(x, y, z, 1 - c))
    n_quads = (NX - 1) * (NY // QUAD)

    with jax.named_scope("slabs"):

        @pl.loop(0, n_quads - 1)
        def _(t):
            add_quad(*await_x(t))

        build(*await_x(n_quads - 1))
        add_side(1 - c)
        swap.start()
        add_side(c)

    with jax.named_scope("cores"):
        swap.wait_recv()

    with jax.named_scope("gains"):
        hist = acc[c] + hist_r[...]
        cols = GROUP * BINS
        src = lax.broadcasted_iota(jnp.int32, (cols, cols), 0)
        dst = lax.broadcasted_iota(jnp.int32, (cols, cols), 1)
        same = (src // BINS) == (dst // BINS)
        upto = jnp.where(same & (src <= dst), 1.0, 0.0).astype(jnp.bfloat16)
        past = jnp.where(same & (src > dst), 1.0, 0.0).astype(jnp.bfloat16)
        left = jnp.zeros_like(hist)
        right = jnp.zeros_like(hist)
        rest = hist
        for _ in range(3):
            piece = rest.astype(jnp.bfloat16)
            rest = rest - piece.astype(jnp.float32)
            left += jnp.dot(piece, upto, preferred_element_type=jnp.float32)
            right += jnp.dot(piece, past, preferred_element_type=jnp.float32)
        for i in range(cols // LANES):
            sums[0, i] = left[:, i * LANES : (i + 1) * LANES]
            sums[1, i] = right[:, i * LANES : (i + 1) * LANES]

        def side_sums(side, lines):
            return jnp.concatenate([sums[side, i, lines, :] for i in range(cols // LANES)], axis=1)

        def squares(get):
            total = jnp.zeros((LEAVES, cols), jnp.float32)
            for k in range(K):
                s = get(pl.ds(k, LEAVES, stride=K))
                total += s * s
            return total / (get(slice(LEAVES * K, LEAVES * K + LEAVES)) + ridge)

        gain = (
            squares(lambda r: side_sums(0, r))
            + squares(lambda r: side_sums(1, r))
            - squares(lambda r: side_sums(0, r) + side_sums(1, r))
        )
        lane = lax.broadcasted_iota(jnp.int32, (1, cols), 1)
        counts = jnp.zeros((1, cols), jnp.int32)
        fetches[5].wait()
        for f in range(GROUP):
            counts = jnp.where(lane // BINS == f, nbins_ref[z * GROUP + f], counts)
        gain = jnp.where(lane % BINS < counts - 1, gain, 0.0)
        for i in range(NZ):
            gain_s[i] = gain[i * LP : (i + 1) * LP]

    def gain_copy(t):
        other = (z + far_first(t, NZ)) % NZ
        return remote(gain_s.at[other], gain_r.at[z], gs_sem.at[t], gr_sem.at[z], dev(x, y, other, c))

    pair = remote(pair_s, pair_r, pair_sem.at[0], pair_sem.at[1], dev(x, y, z, 1 - c))
    plane = [(i, j) for i in range(NX) for j in range(NY) if i or j]
    plane.sort(key=lambda step: -min(step[0], NX - step[0]) - min(step[1], NY - step[1]))
    here = x * NY + y

    def best_copy(t):
        i, j = plane[t]
        device = dev((x + i) % NX, (y + j) % NY, z, c)
        return remote(best_s, best_r.at[here], bs_sem.at[t], br_sem.at[here], device)

    with jax.named_scope("column"):

        @pl.loop(0, NZ - 1)
        def _(t):
            gain_copy(t).start()

        gain_r[z] = gain_s[z]

        @pl.loop(1, NZ)
        def _(i):
            other = (z + i) % NZ
            remote(gain_s.at[0], gain_r.at[other], gs_sem.at[0], gr_sem.at[other], dev(x, y, z, c)).wait_recv()

        best = jnp.max(functools.reduce(jnp.maximum, [gain_r[i] for i in range(NZ)]), axis=1, keepdims=True)
        pair_s[...] = jnp.broadcast_to(best, (LP, LANES))

    with jax.named_scope("pair"):
        pair.start()
        pair.wait_recv()
        best_s[...] = jnp.maximum(pair_s[...], pair_r[...])

    with jax.named_scope("plane"):
        for t in range(NX * NY - 1):
            best_copy(t).start()
        best_r[here] = best_s[...]

        @pl.loop(1, NX * NY)
        def _(i):
            other = (here + i) % (NX * NY)
            remote(best_s, best_r.at[other], bs_sem.at[0], br_sem.at[other], dev(x, y, z, c)).wait_recv()

        best = functools.reduce(jnp.maximum, [best_r[i] for i in range(NX * NY)])[:, :1]
        for i in range(NZ):
            out_ref[:, i * cols : (i + 1) * cols] = gain_r[i] / (best + epsilon)

    with jax.named_scope("sends"):

        @pl.loop(0, NZ)
        def _(i):
            column_values(i, "wait")
            column_bins(i, "wait")

        @pl.loop(0, NY - 1)
        def _(t):
            for copy in y_copies(t):
                copy.wait_send()

        @pl.loop(0, NY)
        def _(ys):
            @pl.loop(0, NX - 1)
            def _(t):
                for copy in x_copies(t, ys):
                    copy.wait_send()

        swap.wait_send()
        pair.wait_send()

        @pl.loop(0, NZ - 1)
        def _(t):
            gain_copy(t).wait_send()

        for t in range(NX * NY - 1):
            best_copy(t).wait_send()


def on_device(NX, NY, NZ, logits, labels, projection, bins, nbins, leaf):
    bf16, f32 = jnp.bfloat16, jnp.float32
    HZ = NZ // 2
    LP = LEAVES // NZ
    rows, classes = logits.shape
    span = HZ * LANES
    cols = GROUP * BINS
    tall = LEAVES * (K + 1)
    VMEM, DMA = pltpu.VMEM, pltpu.SemaphoreType.DMA
    vmem = pl.BlockSpec(memory_space=pltpu.VMEM)
    hbm = pl.BlockSpec(memory_space=pl.ANY)
    half = NX * NY // 2
    bin_block = (GROUP * NX, NY * LANES)
    return pl.pallas_call(
        functools.partial(kernel, NX, NY, NZ),
        out_shape=jax.ShapeDtypeStruct((LP, NZ * cols), f32),
        in_specs=[hbm] * 6,
        out_specs=vmem,
        scratch_shapes=[
            VMEM(logits.shape, bf16),
            VMEM((1, rows), jnp.int32),
            VMEM((K, classes), bf16),
            VMEM(bins.shape, jnp.int32),
            pltpu.SMEM(nbins.shape, jnp.int32),
            VMEM((2 * half, LANES), jnp.int32),
            VMEM((2 * rows, classes), bf16),
            VMEM((NZ, *bin_block), bf16),
            VMEM((half, LANES), bf16),
            VMEM((K, LANES), bf16),
            VMEM((1, LANES), f32),
            VMEM((NZ, *bin_block), bf16),
            VMEM((NZ, half, LANES), bf16),
            VMEM((NZ, K, LANES), bf16),
            VMEM((NZ, 1, LANES), f32),
            VMEM((NZ, NY, GROUP * NX, LANES), f32),
            VMEM((HZ, 2 * half, LANES), f32),
            VMEM((NX, NY, K, span), bf16),
            VMEM((NX, NY, 1, span), f32),
            VMEM((tall, QUAD * span), bf16),
            VMEM((2, cols, QUAD * span), bf16),
            VMEM((2, tall, cols), f32),
            VMEM((tall, cols), f32),
            VMEM((2, cols // LANES, tall, LANES), f32),
            VMEM((NZ, LP, cols), f32),
            VMEM((NZ, LP, cols), f32),
            VMEM((LP, LANES), f32),
            VMEM((LP, LANES), f32),
            VMEM((LP, LANES), f32),
            VMEM((NX * NY, LP, LANES), f32),
            DMA((6,)),
            DMA((4, NZ)),
            DMA((4, NZ)),
            DMA((2, NY)),
            DMA((NY, 2)),
            DMA((NX, 2, NY)),
            DMA((NX, NY, 2)),
            DMA((2,)),
            DMA((NZ,)),
            DMA((NZ,)),
            DMA((2,)),
            DMA((NX * NY,)),
            DMA((NX * NY,)),
        ],
        compiler_params=pltpu.CompilerParams(
            collective_id=0, has_side_effects=True, vmem_limit_bytes=62 * 2**20
        ),
        cost_estimate=pl.CostEstimate(
            flops=2 * tall * 2 * cols * NX * NY * span, bytes_accessed=2**20, transcendentals=rows * classes
        ),
    )(
        logits,
        labels.reshape(1, rows),
        projection.T,
        bins,
        nbins,
        leaf.reshape(2 * half, LANES),
    )


def solution(mesh, NX=4, NY=8):
    return jax.shard_map(
        functools.partial(on_device, NX, NY, mesh.shape["row"]),
        mesh=mesh,
        in_specs=(
            P(("row", "feat"), None),
            P(("row", "feat")),
            P(),
            P("feat", "row"),
            P("feat"),
            P("row"),
        ),
        out_specs=P("row", "feat"),
        check_vma=False,
    )
```

```python
import functools

import jax
import jax.numpy as jnp
from jax import lax
from jax.experimental import pallas as pl
from jax.experimental.pallas import tpu as pltpu
from jax.sharding import PartitionSpec as P

BINS = 64
LEAVES = 16
K = 16
GROUP = 4
QUAD = 4
LANES = 128
MESH = pl.DeviceIdType.MESH
NT = (((1,), (1,)), ((), ()))

ridge = 1.0
epsilon = 1e-6


def near_first(t):
    return ((t + 1) // 2) * (2 * (t % 2) - 1)


def far_first(t, n):
    return n // 2 + near_first(t)


def kernel(
    NX,
    NY,
    NZ,
    logits_any,
    labels_any,
    proj_any,
    bins_any,
    nbins_any,
    leaf_any,
    out_ref,
    logits_v,
    labels_ref,
    proj_ref,
    bins_v,
    nbins_ref,
    leaf_ref,
    grad,
    bins_s,
    rows_s,
    bins_r,
    rows_r,
    bins_f,
    leaf_f,
    vals,
    weights,
    onehot,
    acc,
    hist_r,
    sums,
    gain_s,
    gain_r,
    pair_s,
    pair_r,
    best_s,
    best_r,
    local_sem,
    column_sem,
    send_sem,
    y_sem,
    x_sem,
    swap_sem,
    gain_sem,
    pair_sem,
    best_sem,
):
    HZ = NZ // 2
    LP = LEAVES // NZ
    rows = labels_ref.shape[1]
    z = lax.axis_index("row")
    feat = lax.axis_index("feat")
    c = feat % 2
    y = (feat // 2) % NY
    x = feat // (2 * NY)
    h = z // HZ
    slot = (z % HZ) * 2 + c

    def dev(x_, y_, z_, c_):
        return (z_, (x_ * NY + y_) * 2 + c_)

    def remote(src, dst, send, recv, device):
        return pltpu.make_async_remote_copy(
            src_ref=src, dst_ref=dst, send_sem=send, recv_sem=recv, device_id=device, device_id_type=MESH
        )

    operands = (
        (bins_any, bins_v),
        (logits_any, logits_v),
        (labels_any, labels_ref),
        (proj_any, proj_ref),
        (leaf_any, leaf_ref),
        (nbins_any, nbins_ref),
    )
    fetches = [pltpu.make_async_copy(src, dst, local_sem.at[i]) for i, (src, dst) in enumerate(operands)]
    for fetch in fetches:
        fetch.start()

    barrier = pltpu.get_barrier_semaphore()

    def greet(device):
        pl.semaphore_signal(barrier, inc=1, device_id=device, device_id_type=MESH)

    @pl.loop(1, 2 * NZ)
    def _(i):
        other = (z * 2 + c + i) % (2 * NZ)
        greet(dev(x, y, other // 2, other % 2))

    @pl.loop(1, NY)
    def _(i):
        greet(dev(x, (y + i) % NY, z, c))

    @pl.loop(1, NX)
    def _(i):
        greet(dev((x + i) % NX, y, z, c))

    with jax.named_scope("softmax"):
        for fetch in fetches[1:4]:
            fetch.wait()
        lane = lax.broadcasted_iota(jnp.int32, (rows, rows), 1)
        line = lax.broadcasted_iota(jnp.int32, (rows, rows), 0)
        spread = jnp.where(lane == line, labels_ref[...].astype(jnp.float32), 0.0)
        target = jnp.sum(spread, axis=1, keepdims=True).astype(jnp.int32)
        scores = logits_v[...].astype(jnp.float32)
        highest = jnp.max(scores, axis=1, keepdims=True)
        expd = jnp.exp(scores - highest)
        probability = expd * (1.0 / jnp.sum(expd, axis=1, keepdims=True))
        classes = lax.broadcasted_iota(jnp.int32, scores.shape, 1)
        gradient = probability - jnp.where(classes == target, 1.0, 0.0)
        grad[...] = jnp.zeros_like(grad)
        grad[pl.ds(pl.multiple_of(c * rows, rows), rows), :] = gradient.astype(jnp.bfloat16)
        sketch = lax.dot_general(proj_ref[...], grad[...], NT, preferred_element_type=jnp.float32)
        rows_s[:, :LANES] = sketch.astype(jnp.bfloat16)
        hessian = jnp.sum(probability * (1.0 - probability), axis=1, keepdims=True)
        lane = lax.broadcasted_iota(jnp.int32, (rows, LANES), 1)
        line = lax.broadcasted_iota(jnp.int32, (rows, LANES), 0)
        hessian = jnp.sum(jnp.where(lane == line + c * rows, hessian, 0.0), axis=0, keepdims=True)
        rows_s[:, LANES:] = jnp.broadcast_to(hessian, (K, LANES)).astype(jnp.bfloat16)

    with jax.named_scope("regroup"):
        fetches[0].wait()
        fetches[4].wait()
        width = NY * LANES
        half = NX * NY // 2
        leaf = leaf_ref[pl.ds(pl.multiple_of(c * half, half), half), :].astype(jnp.float32).astype(jnp.bfloat16)
        for d in range(NZ):
            four = bins_v[d * GROUP : (d + 1) * GROUP, :].astype(jnp.float32)
            bins_s[d, :, :width] = jnp.concatenate(
                [four[:, i * width : (i + 1) * width] for i in range(NX)], axis=0
            ).astype(jnp.bfloat16)
            bins_s[d, :half, width:] = leaf

    with jax.named_scope("barrier"):
        pl.semaphore_wait(barrier, 2 * NZ - 1 + NY - 1 + NX - 1)

    def to_column(t, src, dst, kind, act):
        device = dev(x, y, (z + far_first(t, NZ)) % NZ, h)
        here = (t == NZ - 1) & (c == h)

        @pl.when(here)
        def _():
            if act == "start":
                pltpu.make_async_copy(src, dst, column_sem.at[kind]).start()

        @pl.when(jnp.logical_not(here))
        def _():
            copy = remote(src, dst, send_sem.at[kind], column_sem.at[kind], device)
            if act == "start":
                copy.start()
            else:
                copy.wait_send()

    def column_values(t, act):
        to_column(t, rows_s, rows_r.at[slot], 0, act)

    def column_bins(t, act):
        to_column(t, bins_s.at[(z + far_first(t, NZ)) % NZ], bins_r.at[slot], 1, act)

    @pl.loop(0, NZ)
    def _(t):
        column_values(t, "start")

    @pl.loop(0, NZ)
    def _(t):
        column_bins(t, "start")

    def await_bytes(ref, sem):
        pltpu.make_async_copy(ref, ref, sem).wait()

    with jax.named_scope("zvalues"):
        await_bytes(rows_r, column_sem.at[0])
        first = lax.broadcasted_iota(jnp.int32, (1, LANES), 1) < rows
        line = lax.broadcasted_iota(jnp.int32, (K, LANES), 0)
        hessians = jnp.zeros((K, LANES), jnp.float32)
        for i in range(HZ):
            both = [rows_r[2 * i + j].astype(jnp.float32) for j in range(2)]
            merged = jnp.where(first, both[0][:, :LANES], both[1][:, :LANES])
            vals[x, y, :, i * LANES : (i + 1) * LANES] = merged.astype(jnp.bfloat16)
            merged = jnp.where(first, both[0][:, LANES:], both[1][:, LANES:])
            hessians = jnp.where(line == i, merged, hessians)
        vals[x, y, :, HZ * LANES :] = hessians.astype(jnp.bfloat16)

    def y_copy(t):
        device = dev(x, (y + far_first(t, NY)) % NY, z, c)
        return remote(vals.at[x, y], vals.at[x, y], send_sem.at[2], y_sem.at[y], device)

    def x_copy(t, ys, quad):
        device = dev((x + far_first(t, NX)) % NX, y, z, c)
        return remote(vals.at[x, ys], vals.at[x, ys], send_sem.at[3], x_sem.at[x, quad], device)

    def forward(ys, quad):
        @pl.loop(0, NX - 1)
        def _(t):
            x_copy(t, ys, quad).start()

    @pl.loop(0, NY - 1)
    def _(t):
        y_copy(t).start()

    forward(y, 0)
    acc[...] = jnp.zeros_like(acc)

    def near_y(t):
        return (y + near_first(t) + NY) % NY

    def await_y(t):
        ys = near_y(t)
        await_bytes(vals.at[x, ys], y_sem.at[ys])
        forward(ys, t // QUAD)

    pl.loop(1, QUAD)(await_y)

    with jax.named_scope("zbins"):
        await_bytes(bins_r, column_sem.at[1])
        for i in range(2 * HZ):
            for j in range(NY):
                bins_f[i, j] = bins_r[i, :, j * LANES : (j + 1) * LANES].astype(jnp.float32)
            leaf_f[i // 2, (i % 2) * half : (i % 2 + 1) * half] = bins_r[i, :half, width:].astype(jnp.float32)

    bin_ids = lax.broadcasted_iota(jnp.int32, (BINS, LANES), 0).astype(jnp.float32).astype(jnp.bfloat16)
    leaf_ids = lax.broadcasted_iota(jnp.int32, (LEAVES, LANES), 0).astype(jnp.float32).astype(jnp.bfloat16)
    one, nil = jnp.bfloat16(1), jnp.bfloat16(0)

    def build(xs, quad):
        for b in range(QUAD):
            ys = near_y(quad * QUAD + b)
            hessians = vals[xs, ys, :, HZ * LANES :].astype(jnp.float32)
            for i in range(HZ):
                src = slice(i * LANES, (i + 1) * LANES)
                dst = slice((b * HZ + i) * LANES, (b * HZ + i + 1) * LANES)
                leaf = leaf_f[i, pl.ds(xs * NY + ys, 1), :]
                leaf = jnp.broadcast_to(leaf, (LEAVES, LANES)).astype(jnp.bfloat16)
                tile = vals[xs, ys, :, src]
                for l in range(LEAVES):
                    weights[l * K : (l + 1) * K, dst] = jnp.where(leaf == jnp.bfloat16(l), tile, nil)
                hess = jnp.broadcast_to(hessians[i : i + 1], (LEAVES, LANES)).astype(jnp.bfloat16)
                weights[LEAVES * K :, dst] = jnp.where(leaf == leaf_ids, hess, nil)
                for side in range(2):
                    for f in range(GROUP):
                        ids = bins_f[2 * i + side, ys, pl.ds(xs * GROUP + f, 1), :]
                        ids = jnp.broadcast_to(ids, (BINS, LANES)).astype(jnp.bfloat16)
                        onehot[side, f * BINS : (f + 1) * BINS, dst] = jnp.where(ids == bin_ids, one, nil)

    def add_side(side):
        acc[side] += lax.dot_general(weights[...], onehot[side], NT, preferred_element_type=jnp.float32)

    def add_quad(xs, quad):
        build(xs, quad)
        add_side(0)
        add_side(1)

    with jax.named_scope("ownslab"):

        @pl.loop(0, NY // QUAD)
        def _(quad):
            @pl.when(quad > 0)
            def _():
                pl.loop(quad * QUAD, (quad + 1) * QUAD)(await_y)

            add_quad(x, quad)

    def await_x(t):
        quad, xs = t // (NX - 1), (x + near_first(t % (NX - 1) + 1) + NX) % NX

        await_bytes(vals.at[xs, pl.ds(0, QUAD)], x_sem.at[xs, quad])
        return xs, quad

    swap = remote(acc.at[1 - c], hist_r, swap_sem.at[0], swap_sem.at[1], dev(x, y, z, 1 - c))
    n_quads = (NX - 1) * (NY // QUAD)

    with jax.named_scope("slabs"):

        @pl.loop(0, n_quads - 1)
        def _(t):
            add_quad(*await_x(t))

        build(*await_x(n_quads - 1))
        add_side(1 - c)
        swap.start()
        add_side(c)

    with jax.named_scope("cores"):
        swap.wait_recv()

    with jax.named_scope("gains"):
        hist = acc[c] + hist_r[...]
        cols = GROUP * BINS
        src = lax.broadcasted_iota(jnp.int32, (cols, cols), 0)
        dst = lax.broadcasted_iota(jnp.int32, (cols, cols), 1)
        same = (src // BINS) == (dst // BINS)
        upto = jnp.where(same & (src <= dst), 1.0, 0.0).astype(jnp.bfloat16)
        past = jnp.where(same & (src > dst), 1.0, 0.0).astype(jnp.bfloat16)
        left = jnp.zeros_like(hist)
        right = jnp.zeros_like(hist)
        rest = hist
        for _ in range(3):
            piece = rest.astype(jnp.bfloat16)
            rest = rest - piece.astype(jnp.float32)
            left += jnp.dot(piece, upto, preferred_element_type=jnp.float32)
            right += jnp.dot(piece, past, preferred_element_type=jnp.float32)
        for i in range(cols // LANES):
            sums[0, i] = left[:, i * LANES : (i + 1) * LANES]
            sums[1, i] = right[:, i * LANES : (i + 1) * LANES]

        def side_sums(side, lines):
            return jnp.concatenate([sums[side, i, lines, :] for i in range(cols // LANES)], axis=1)

        def squares(get):
            total = jnp.zeros((LEAVES, cols), jnp.float32)
            for k in range(K):
                s = get(pl.ds(k, LEAVES, stride=K))
                total += s * s
            return total / (get(slice(LEAVES * K, LEAVES * K + LEAVES)) + ridge)

        gain = (
            squares(lambda r: side_sums(0, r))
            + squares(lambda r: side_sums(1, r))
            - squares(lambda r: side_sums(0, r) + side_sums(1, r))
        )
        lane = lax.broadcasted_iota(jnp.int32, (1, cols), 1)
        counts = jnp.zeros((1, cols), jnp.int32)
        fetches[5].wait()
        for f in range(GROUP):
            counts = jnp.where(lane // BINS == f, nbins_ref[z * GROUP + f], counts)
        gain = jnp.where(lane % BINS < counts - 1, gain, 0.0)
        for i in range(NZ):
            gain_s[i] = gain[i * LP : (i + 1) * LP]

    def gain_copy(t):
        other = (z + far_first(t, NZ)) % NZ
        return remote(gain_s.at[other], gain_r.at[z], gain_sem.at[0], gain_sem.at[1], dev(x, y, other, c))

    pair = remote(pair_s, pair_r, pair_sem.at[0], pair_sem.at[1], dev(x, y, z, 1 - c))
    plane = [(i, j) for i in range(NX) for j in range(NY) if i or j]
    plane.sort(key=lambda step: -min(step[0], NX - step[0]) - min(step[1], NY - step[1]))
    here = x * NY + y

    def best_copy(t):
        i, j = plane[t]
        device = dev((x + i) % NX, (y + j) % NY, z, c)
        return remote(best_s, best_r.at[here], best_sem.at[0], best_sem.at[1], device)

    with jax.named_scope("column"):

        @pl.loop(0, NZ - 1)
        def _(t):
            gain_copy(t).start()

        gain_r[z] = gain_s[z]

        await_bytes(gain_r.at[pl.ds(0, NZ - 1)], gain_sem.at[1])
        best = jnp.max(functools.reduce(jnp.maximum, [gain_r[i] for i in range(NZ)]), axis=1, keepdims=True)
        pair_s[...] = jnp.broadcast_to(best, (LP, LANES))

    with jax.named_scope("pair"):
        pair.start()
        pair.wait_recv()
        best_s[...] = jnp.maximum(pair_s[...], pair_r[...])

    with jax.named_scope("plane"):
        for t in range(NX * NY - 1):
            best_copy(t).start()
        best_r[here] = best_s[...]

        await_bytes(best_r.at[pl.ds(0, NX * NY - 1)], best_sem.at[1])
        best = functools.reduce(jnp.maximum, [best_r[i] for i in range(NX * NY)])[:, :1]
        for i in range(NZ):
            out_ref[:, i * cols : (i + 1) * cols] = gain_r[i] / (best + epsilon)

    with jax.named_scope("sends"):

        @pl.loop(0, NZ)
        def _(t):
            column_values(t, "wait")
            column_bins(t, "wait")

        await_bytes(vals.at[0, pl.ds(0, NY - 1)], send_sem.at[2])
        await_bytes(vals.at[pl.ds(0, NX - 1)], send_sem.at[3])
        swap.wait_send()
        pair.wait_send()
        await_bytes(gain_s.at[pl.ds(0, NZ - 1)], gain_sem.at[0])
        await_bytes(best_r.at[pl.ds(0, NX * NY - 1)], best_sem.at[0])


def on_device(NX, NY, NZ, logits, labels, projection, bins, nbins, leaf):
    bf16, f32 = jnp.bfloat16, jnp.float32
    HZ = NZ // 2
    LP = LEAVES // NZ
    rows, classes = logits.shape
    span = HZ * LANES
    cols = GROUP * BINS
    tall = LEAVES * (K + 1)
    VMEM, DMA = pltpu.VMEM, pltpu.SemaphoreType.DMA
    vmem = pl.BlockSpec(memory_space=pltpu.VMEM)
    hbm = pl.BlockSpec(memory_space=pl.ANY)
    half = NX * NY // 2
    bin_block = (GROUP * NX, (NY + 1) * LANES)
    return pl.pallas_call(
        functools.partial(kernel, NX, NY, NZ),
        out_shape=jax.ShapeDtypeStruct((LP, NZ * cols), f32),
        in_specs=[hbm] * 6,
        out_specs=vmem,
        scratch_shapes=[
            VMEM(logits.shape, bf16),
            VMEM((1, rows), jnp.int32),
            VMEM((K, classes), bf16),
            VMEM(bins.shape, jnp.int32),
            pltpu.SMEM(nbins.shape, jnp.int32),
            VMEM((2 * half, LANES), jnp.int32),
            VMEM((2 * rows, classes), bf16),
            VMEM((NZ, *bin_block), bf16),
            VMEM((K, 2 * LANES), bf16),
            VMEM((NZ, *bin_block), bf16),
            VMEM((NZ, K, 2 * LANES), bf16),
            VMEM((NZ, NY, GROUP * NX, LANES), f32),
            VMEM((HZ, 2 * half, LANES), f32),
            VMEM((NX, NY, K, span + LANES), bf16),
            VMEM((tall, QUAD * span), bf16),
            VMEM((2, cols, QUAD * span), bf16),
            VMEM((2, tall, cols), f32),
            VMEM((tall, cols), f32),
            VMEM((2, cols // LANES, tall, LANES), f32),
            VMEM((NZ, LP, cols), f32),
            VMEM((NZ, LP, cols), f32),
            VMEM((LP, LANES), f32),
            VMEM((LP, LANES), f32),
            VMEM((LP, LANES), f32),
            VMEM((NX * NY, LP, LANES), f32),
            DMA((6,)),
            DMA((2,)),
            DMA((4,)),
            DMA((NY,)),
            DMA((NX, NY // QUAD)),
            DMA((2,)),
            DMA((2,)),
            DMA((2,)),
            DMA((2,)),
        ],
        compiler_params=pltpu.CompilerParams(
            collective_id=0, has_side_effects=True, vmem_limit_bytes=62 * 2**20
        ),
        cost_estimate=pl.CostEstimate(
            flops=2 * tall * 2 * cols * NX * NY * span, bytes_accessed=2**20, transcendentals=rows * classes
        ),
    )(
        logits,
        labels.reshape(1, rows),
        projection.T,
        bins,
        nbins,
        leaf.reshape(2 * half, LANES),
    )


def solution(mesh, NX=4, NY=8):
    return jax.shard_map(
        functools.partial(on_device, NX, NY, mesh.shape["row"]),
        mesh=mesh,
        in_specs=(
            P(("row", "feat"), None),
            P(("row", "feat")),
            P(),
            P("feat", "row"),
            P("feat"),
            P("row"),
        ),
        out_specs=P("row", "feat"),
        check_vma=False,
    )
```

```python
import functools

import jax
import jax.numpy as jnp
from jax import lax
from jax.experimental import pallas as pl
from jax.experimental.pallas import tpu as pltpu
from jax.sharding import PartitionSpec as P

BINS = 64
LEAVES = 16
K = 16
GROUP = 4
QUAD = 4
LANES = 128
MESH = pl.DeviceIdType.MESH
NT = (((1,), (1,)), ((), ()))

ridge = 1.0
epsilon = 1e-6


def near_first(t):
    return ((t + 1) // 2) * (2 * (t % 2) - 1)


def far_first(t, n):
    return n // 2 + near_first(t)


def kernel(
    NX,
    NY,
    NZ,
    logits_any,
    labels_any,
    proj_any,
    bins_any,
    nbins_any,
    leaf_any,
    out_ref,
    logits_v,
    labels_ref,
    proj_ref,
    bins_v,
    nbins_ref,
    leaf_ref,
    grad,
    bins_s,
    rows_s,
    bins_r,
    rows_r,
    bins_f,
    vals,
    weights,
    onehot,
    acc,
    hist_r,
    sums,
    gain_s,
    gain_r,
    peak_s,
    peak_r,
    best_s,
    best_r,
    local_sem,
    column_sem,
    send_sem,
    y_sem,
    x_sem,
    swap_sem,
    gain_sem,
    peak_sem,
    best_sem,
):
    HZ = NZ // 2
    LP = LEAVES // NZ
    rows = labels_ref.shape[1]
    z = lax.axis_index("row")
    feat = lax.axis_index("feat")
    c = feat % 2
    y = (feat // 2) % NY
    x = feat // (2 * NY)
    h = z // HZ
    slot = (z % HZ) * 2 + c

    def dev(x_, y_, z_, c_):
        return (z_, (x_ * NY + y_) * 2 + c_)

    def remote(src, dst, send, recv, device):
        return pltpu.make_async_remote_copy(
            src_ref=src, dst_ref=dst, send_sem=send, recv_sem=recv, device_id=device, device_id_type=MESH
        )

    operands = (
        (bins_any, bins_v),
        (logits_any, logits_v),
        (labels_any, labels_ref),
        (proj_any, proj_ref),
        (leaf_any, leaf_ref),
        (nbins_any, nbins_ref),
    )
    fetches = [pltpu.make_async_copy(src, dst, local_sem.at[i]) for i, (src, dst) in enumerate(operands)]
    for fetch in fetches:
        fetch.start()

    barrier = pltpu.get_barrier_semaphore()

    def greet(device):
        pl.semaphore_signal(barrier, inc=1, device_id=device, device_id_type=MESH)

    for t in range(max(NX, NY, NZ)):
        if t < NZ:
            other = (z + far_first(t, NZ)) % NZ
            greet(dev(x, y, other, 1 - c))
            if t < NZ - 1:
                greet(dev(x, y, other, c))
        if t < NY - 1:
            greet(dev(x, (y + far_first(t, NY)) % NY, z, c))
        if t < NX - 1:
            greet(dev((x + far_first(t, NX)) % NX, y, z, c))

    with jax.named_scope("softmax"):
        for fetch in fetches[1:5]:
            fetch.wait()
        lane = lax.broadcasted_iota(jnp.int32, (rows, rows), 1)
        line = lax.broadcasted_iota(jnp.int32, (rows, rows), 0)
        spread = jnp.where(lane == line, labels_ref[...].astype(jnp.float32), 0.0)
        target = jnp.sum(spread, axis=1, keepdims=True).astype(jnp.int32)
        scores = logits_v[...].astype(jnp.float32)
        highest = jnp.max(scores, axis=1, keepdims=True)
        expd = jnp.exp(scores - highest)
        probability = expd * (1.0 / jnp.sum(expd, axis=1, keepdims=True))
        classes = lax.broadcasted_iota(jnp.int32, scores.shape, 1)
        gradient = probability - jnp.where(classes == target, 1.0, 0.0)
        grad[...] = jnp.zeros_like(grad)
        grad[pl.ds(pl.multiple_of(c * rows, rows), rows), :] = gradient.astype(jnp.bfloat16)
        sketch = lax.dot_general(proj_ref[...], grad[...], NT, preferred_element_type=jnp.float32)
        hessian = jnp.sum(probability * (1.0 - probability), axis=1, keepdims=True)
        lane = lax.broadcasted_iota(jnp.int32, (rows, LANES), 1)
        line = lax.broadcasted_iota(jnp.int32, (rows, LANES), 0)
        hessian = jnp.sum(jnp.where(lane == line + (1 - c) * rows, hessian, 0.0), axis=0, keepdims=True)
        leaf = pltpu.roll(leaf_ref[pl.ds(x * NY + y, 1), :].astype(jnp.float32), rows, 1)
        lane = lax.broadcasted_iota(jnp.int32, (K, LANES), 1)
        line = lax.broadcasted_iota(jnp.int32, (K, LANES), 0)
        beside = jnp.where(line == 0, hessian, jnp.where(line == 1, leaf, 0.0))
        rows_s[...] = jnp.where(lane // rows == c, sketch, beside).astype(jnp.bfloat16)

    with jax.named_scope("regroup"):
        fetches[0].wait()
        width = NY * LANES
        for d in range(NZ):
            four = bins_v[d * GROUP : (d + 1) * GROUP, :].astype(jnp.float32)
            bins_s[d] = jnp.concatenate(
                [four[:, i * width : (i + 1) * width] for i in range(NX)], axis=0
            ).astype(jnp.bfloat16)

    with jax.named_scope("barrier"):
        pl.semaphore_wait(barrier, 2 * NZ - 1 + NY - 1 + NX - 1)

    def to_column(t, src, dst, kind, act):
        device = dev(x, y, (z + far_first(t, NZ)) % NZ, h)
        here = (t == NZ - 1) & (c == h)

        @pl.when(here)
        def _():
            if act == "start":
                pltpu.make_async_copy(src, dst, column_sem.at[kind]).start()

        @pl.when(jnp.logical_not(here))
        def _():
            copy = remote(src, dst, send_sem.at[kind], column_sem.at[kind], device)
            if act == "start":
                copy.start()
            else:
                copy.wait_send()

    def column_values(t, act):
        to_column(t, rows_s, rows_r.at[slot], 0, act)

    def column_bins(t, act):
        to_column(t, bins_s.at[(z + far_first(t, NZ)) % NZ], bins_r.at[slot], 1, act)

    @pl.loop(0, NZ)
    def _(t):
        column_values(t, "start")

    @pl.loop(0, NZ)
    def _(t):
        column_bins(t, "start")

    def await_bytes(ref, sem):
        pltpu.make_async_copy(ref, ref, sem).wait()

    with jax.named_scope("zvalues"):
        await_bytes(rows_r, column_sem.at[0])
        first = lax.broadcasted_iota(jnp.int32, (1, LANES), 1) < rows
        line = lax.broadcasted_iota(jnp.int32, (K, LANES), 0)
        beside = jnp.zeros((K, LANES), jnp.float32)
        for i in range(HZ):
            low, high = rows_r[2 * i].astype(jnp.float32), rows_r[2 * i + 1].astype(jnp.float32)
            vals[x, y, :, i * LANES : (i + 1) * LANES] = jnp.where(first, low, high).astype(jnp.bfloat16)
            other = pltpu.roll(jnp.where(first, high, low), rows, 1)
            beside = jnp.where(line == i, other[0:1], jnp.where(line == HZ + i, other[1:2], beside))
        vals[x, y, :, HZ * LANES :] = beside.astype(jnp.bfloat16)

    def y_copy(t):
        device = dev(x, (y + far_first(t, NY)) % NY, z, c)
        return remote(vals.at[x, y], vals.at[x, y], send_sem.at[2], y_sem.at[y], device)

    def x_copy(t, ys, quad):
        device = dev((x + far_first(t, NX)) % NX, y, z, c)
        return remote(vals.at[x, ys], vals.at[x, ys], send_sem.at[3], x_sem.at[x, quad], device)

    def forward(ys, quad):
        @pl.loop(0, NX - 1)
        def _(t):
            x_copy(t, ys, quad).start()

    @pl.loop(0, NY - 1)
    def _(t):
        y_copy(t).start()

    forward(y, 0)
    acc[...] = jnp.zeros_like(acc)

    def near_y(t):
        return (y + near_first(t) + NY) % NY

    def await_y(t):
        ys = near_y(t)
        await_bytes(vals.at[x, ys], y_sem.at[ys])
        forward(ys, t // QUAD)

    pl.loop(1, NY)(await_y)

    with jax.named_scope("zbins"):
        await_bytes(bins_r, column_sem.at[1])
        for i in range(2 * HZ):
            for j in range(NY):
                bins_f[i, j] = bins_r[i, :, j * LANES : (j + 1) * LANES].astype(jnp.float32)

    bin_ids = lax.broadcasted_iota(jnp.int32, (BINS, LANES), 0).astype(jnp.float32).astype(jnp.bfloat16)
    leaf_ids = lax.broadcasted_iota(jnp.int32, (LEAVES, LANES), 0).astype(jnp.float32).astype(jnp.bfloat16)
    one, nil = jnp.bfloat16(1), jnp.bfloat16(0)

    def build(part, xs, quad):
        for b in range(QUAD):
            ys = near_y(quad * QUAD + b)
            beside = vals[xs, ys, :, HZ * LANES :].astype(jnp.float32)
            for i in range(HZ):
                src = slice(i * LANES, (i + 1) * LANES)
                at = ((part * QUAD + b) * HZ + i) * LANES
                dst = slice(at, at + LANES)
                hess = jnp.broadcast_to(beside[i : i + 1], (LEAVES, LANES)).astype(jnp.bfloat16)
                leaf = jnp.broadcast_to(beside[HZ + i : HZ + i + 1], (LEAVES, LANES)).astype(jnp.bfloat16)
                tile = vals[xs, ys, :, src]
                for l in range(LEAVES):
                    weights[l * K : (l + 1) * K, dst] = jnp.where(leaf == jnp.bfloat16(l), tile, nil)
                weights[LEAVES * K :, dst] = jnp.where(leaf == leaf_ids, hess, nil)
                for side in range(2):
                    for f in range(GROUP):
                        ids = bins_f[2 * i + side, ys, pl.ds(xs * GROUP + f, 1), :]
                        ids = jnp.broadcast_to(ids, (BINS, LANES)).astype(jnp.bfloat16)
                        onehot[side, f * BINS : (f + 1) * BINS, dst] = jnp.where(ids == bin_ids, one, nil)

    def add_side(parts, side):
        depth = slice(0, parts * QUAD * HZ * LANES)
        acc[side] += lax.dot_general(weights[:, depth], onehot[side, :, depth], NT, preferred_element_type=jnp.float32)

    def add_both(parts):
        add_side(parts, 0)
        add_side(parts, 1)

    with jax.named_scope("ownslab"):
        for quad in range(NY // QUAD):
            build(quad, x, quad)
        add_both(NY // QUAD)

    def await_x(t):
        quad, xs = t // (NX - 1), (x + near_first(t % (NX - 1) + 1) + NX) % NX

        await_bytes(vals.at[xs, pl.ds(0, QUAD)], x_sem.at[xs, quad])
        return xs, quad

    swap = remote(acc.at[1 - c], hist_r, swap_sem.at[0], swap_sem.at[1], dev(x, y, z, 1 - c))
    n_quads = (NX - 1) * (NY // QUAD)

    with jax.named_scope("slabs"):

        @pl.loop(0, (n_quads - 1) // 2)
        def _(t):
            build(0, *await_x(2 * t))
            build(1, *await_x(2 * t + 1))
            add_both(2)

        for t in range((n_quads - 1) // 2 * 2, n_quads - 1):
            build(0, *await_x(t))
            add_both(1)

        build(0, *await_x(n_quads - 1))
        add_side(1, 1 - c)
        swap.start()
        add_side(1, c)

    with jax.named_scope("cores"):
        swap.wait_recv()

    with jax.named_scope("gains"):
        hist = acc[c] + hist_r[...]
        cols = GROUP * BINS
        src = lax.broadcasted_iota(jnp.int32, (cols, cols), 0)
        dst = lax.broadcasted_iota(jnp.int32, (cols, cols), 1)
        same = (src // BINS) == (dst // BINS)
        upto = jnp.where(same & (src <= dst), 1.0, 0.0).astype(jnp.bfloat16)
        past = jnp.where(same & (src > dst), 1.0, 0.0).astype(jnp.bfloat16)
        left = jnp.zeros_like(hist)
        right = jnp.zeros_like(hist)
        rest = hist
        for _ in range(3):
            piece = rest.astype(jnp.bfloat16)
            rest = rest - piece.astype(jnp.float32)
            left += jnp.dot(piece, upto, preferred_element_type=jnp.float32)
            right += jnp.dot(piece, past, preferred_element_type=jnp.float32)
        for i in range(cols // LANES):
            sums[0, i] = left[:, i * LANES : (i + 1) * LANES]
            sums[1, i] = right[:, i * LANES : (i + 1) * LANES]

        def side_sums(side, lines):
            return jnp.concatenate([sums[side, i, lines, :] for i in range(cols // LANES)], axis=1)

        def squares(get):
            total = jnp.zeros((LEAVES, cols), jnp.float32)
            for k in range(K):
                s = get(pl.ds(k, LEAVES, stride=K))
                total += s * s
            return total / (get(slice(LEAVES * K, LEAVES * K + LEAVES)) + ridge)

        gain = (
            squares(lambda r: side_sums(0, r))
            + squares(lambda r: side_sums(1, r))
            - squares(lambda r: side_sums(0, r) + side_sums(1, r))
        )
        lane = lax.broadcasted_iota(jnp.int32, (1, cols), 1)
        counts = jnp.zeros((1, cols), jnp.int32)
        fetches[5].wait()
        for f in range(GROUP):
            counts = jnp.where(lane // BINS == f, nbins_ref[z * GROUP + f], counts)
        gain = jnp.where(lane % BINS < counts - 1, gain, 0.0)
        best = jnp.broadcast_to(jnp.max(gain, axis=1, keepdims=True), (LEAVES, LANES))
        for i in range(NZ):
            gain_s[i] = gain[i * LP : (i + 1) * LP]
            peak_s[i] = best[i * LP : (i + 1) * LP]

    def gain_copy(t):
        other = (z + far_first(t, NZ)) % NZ
        return remote(gain_s.at[other], gain_r.at[z], gain_sem.at[0], gain_sem.at[1], dev(x, y, other, c))

    def peak_copy(t):
        other = (z + far_first(t, NZ)) % NZ
        return remote(peak_s.at[other], peak_r.at[z], peak_sem.at[0], peak_sem.at[1], dev(x, y, other, 1 - c))

    plane = [(i, j) for i in range(NX) for j in range(NY) if i or j]
    plane.sort(key=lambda step: -min(step[0], NX - step[0]) - min(step[1], NY - step[1]))
    here = x * NY + y

    def best_copy(t):
        i, j = plane[t]
        device = dev((x + i) % NX, (y + j) % NY, z, c)
        return remote(best_s, best_r.at[here], best_sem.at[0], best_sem.at[1], device)

    with jax.named_scope("column"):

        @pl.loop(0, NZ - 1)
        def _(t):
            peak_copy(t).start()
            gain_copy(t).start()

        peak_copy(NZ - 1).start()
        gain_r[z] = gain_s[z]

        await_bytes(gain_r.at[pl.ds(0, NZ - 1)], gain_sem.at[1])
        await_bytes(peak_r, peak_sem.at[1])
        best = jnp.max(functools.reduce(jnp.maximum, [gain_r[i] for i in range(NZ)]), axis=1, keepdims=True)
        best_s[...] = functools.reduce(jnp.maximum, [peak_r[i] for i in range(NZ)] + [best])

    with jax.named_scope("plane"):
        for t in range(NX * NY - 1):
            best_copy(t).start()
        best_r[here] = best_s[...]

        await_bytes(best_r.at[pl.ds(0, NX * NY - 1)], best_sem.at[1])
        best = functools.reduce(jnp.maximum, [best_r[i] for i in range(NX * NY)])[:, :1]
        for i in range(NZ):
            out_ref[:, i * cols : (i + 1) * cols] = gain_r[i] / (best + epsilon)

    with jax.named_scope("sends"):

        @pl.loop(0, NZ)
        def _(t):
            column_values(t, "wait")
            column_bins(t, "wait")

        await_bytes(vals.at[0, pl.ds(0, NY - 1)], send_sem.at[2])
        await_bytes(vals.at[pl.ds(0, NX - 1)], send_sem.at[3])
        swap.wait_send()
        await_bytes(peak_s, peak_sem.at[0])
        await_bytes(gain_s.at[pl.ds(0, NZ - 1)], gain_sem.at[0])
        await_bytes(best_r.at[pl.ds(0, NX * NY - 1)], best_sem.at[0])


def on_device(NX, NY, NZ, logits, labels, projection, bins, nbins, leaf):
    bf16, f32 = jnp.bfloat16, jnp.float32
    HZ = NZ // 2
    LP = LEAVES // NZ
    rows, classes = logits.shape
    span = HZ * LANES
    cols = GROUP * BINS
    tall = LEAVES * (K + 1)
    VMEM, DMA = pltpu.VMEM, pltpu.SemaphoreType.DMA
    vmem = pl.BlockSpec(memory_space=pltpu.VMEM)
    hbm = pl.BlockSpec(memory_space=pl.ANY)
    bin_block = (GROUP * NX, NY * LANES)
    return pl.pallas_call(
        functools.partial(kernel, NX, NY, NZ),
        out_shape=jax.ShapeDtypeStruct((LP, NZ * cols), f32),
        in_specs=[hbm] * 6,
        out_specs=vmem,
        scratch_shapes=[
            VMEM(logits.shape, bf16),
            VMEM((1, rows), jnp.int32),
            VMEM((K, classes), bf16),
            VMEM(bins.shape, jnp.int32),
            pltpu.SMEM(nbins.shape, jnp.int32),
            VMEM((NX * NY, LANES), jnp.int32),
            VMEM((2 * rows, classes), bf16),
            VMEM((NZ, *bin_block), bf16),
            VMEM((K, LANES), bf16),
            VMEM((NZ, *bin_block), bf16),
            VMEM((NZ, K, LANES), bf16),
            VMEM((NZ, NY, GROUP * NX, LANES), f32),
            VMEM((NX, NY, K, span + LANES), bf16),
            VMEM((tall, 2 * QUAD * span), bf16),
            VMEM((2, cols, 2 * QUAD * span), bf16),
            VMEM((2, tall, cols), f32),
            VMEM((tall, cols), f32),
            VMEM((2, cols // LANES, tall, LANES), f32),
            VMEM((NZ, LP, cols), f32),
            VMEM((NZ, LP, cols), f32),
            VMEM((NZ, LP, LANES), f32),
            VMEM((NZ, LP, LANES), f32),
            VMEM((LP, LANES), f32),
            VMEM((NX * NY, LP, LANES), f32),
            DMA((6,)),
            DMA((2,)),
            DMA((4,)),
            DMA((NY,)),
            DMA((NX, NY // QUAD)),
            DMA((2,)),
            DMA((2,)),
            DMA((2,)),
            DMA((2,)),
        ],
        compiler_params=pltpu.CompilerParams(
            collective_id=0, has_side_effects=True, vmem_limit_bytes=62 * 2**20
        ),
        cost_estimate=pl.CostEstimate(
            flops=2 * tall * 2 * cols * NX * NY * span, bytes_accessed=2**20, transcendentals=rows * classes
        ),
    )(
        logits,
        labels.reshape(1, rows),
        projection.T,
        bins,
        nbins,
        leaf.reshape(NX * NY, LANES),
    )


def solution(mesh, NX=4, NY=8):
    return jax.shard_map(
        functools.partial(on_device, NX, NY, mesh.shape["row"]),
        mesh=mesh,
        in_specs=(
            P(("row", "feat"), None),
            P(("row", "feat")),
            P(),
            P("feat", "row"),
            P("feat"),
            P("row"),
        ),
        out_specs=P("row", "feat"),
        check_vma=False,
    )
```

```python
import functools

import jax
import jax.numpy as jnp
from jax import lax
from jax.experimental import pallas as pl
from jax.experimental.pallas import tpu as pltpu
from jax.sharding import PartitionSpec as P

BINS = 64
LEAVES = 16
K = 16
GROUP = 4
LANES = 128
MESH = pl.DeviceIdType.MESH
NT = (((1,), (1,)), ((), ()))

ridge = 1.0
epsilon = 1e-6


def near_first(t):
    return ((t + 1) // 2) * (2 * (t % 2) - 1)


def far_first(t, n):
    return n // 2 + near_first(t)


def kernel(
    NX,
    NY,
    NZ,
    logits_any,
    labels_any,
    proj_any,
    bins_any,
    nbins_any,
    leaf_any,
    out_ref,
    logits_v,
    labels_ref,
    proj_ref,
    bins_v,
    nbins_ref,
    leaf_ref,
    grad,
    bins_s,
    rows_s,
    bins_r,
    rows_r,
    bins_f,
    vals,
    weights,
    onehot,
    steps,
    acc,
    hist_r,
    sums,
    gain_s,
    gain_r,
    peak_s,
    peak_r,
    best_s,
    best_r,
    local_sem,
    column_sem,
    send_sem,
    y_sem,
    direct_sem,
    near_sem,
    far_sem,
    swap_sem,
    gain_sem,
    peak_sem,
    best_sem,
):
    HZ = NZ // 2
    LP = LEAVES // NZ
    NEAR = NY // 2
    cols = GROUP * BINS
    rows = labels_ref.shape[1]
    z = lax.axis_index("row")
    feat = lax.axis_index("feat")
    c = feat % 2
    y = (feat // 2) % NY
    x = feat // (2 * NY)
    h = z // HZ
    slot = (z % HZ) * 2 + c

    def dev(x_, y_, z_, c_):
        return (z_, (x_ * NY + y_) * 2 + c_)

    def remote(src, dst, send, recv, device):
        return pltpu.make_async_remote_copy(
            src_ref=src, dst_ref=dst, send_sem=send, recv_sem=recv, device_id=device, device_id_type=MESH
        )

    operands = (
        (bins_any, bins_v),
        (logits_any, logits_v),
        (labels_any, labels_ref),
        (proj_any, proj_ref),
        (leaf_any, leaf_ref),
        (nbins_any, nbins_ref),
    )
    fetches = [pltpu.make_async_copy(src, dst, local_sem.at[i]) for i, (src, dst) in enumerate(operands)]
    for fetch in fetches:
        fetch.start()

    barrier = pltpu.get_barrier_semaphore()

    def greet(device):
        pl.semaphore_signal(barrier, inc=1, device_id=device, device_id_type=MESH)

    for t in range(max(NX, NY, NZ)):
        if t < NZ:
            other = (z + far_first(t, NZ)) % NZ
            greet(dev(x, y, other, 1 - c))
            if t < NZ - 1:
                greet(dev(x, y, other, c))
        if t < NY - 1:
            greet(dev(x, (y + far_first(t, NY)) % NY, z, c))
        if t < NX - 1:
            greet(dev((x + far_first(t, NX)) % NX, y, z, c))

    with jax.named_scope("softmax"):
        for fetch in fetches[1:5]:
            fetch.wait()
        lane = lax.broadcasted_iota(jnp.int32, (rows, rows), 1)
        line = lax.broadcasted_iota(jnp.int32, (rows, rows), 0)
        spread = jnp.where(lane == line, labels_ref[...].astype(jnp.float32), 0.0)
        target = jnp.sum(spread, axis=1, keepdims=True).astype(jnp.int32)
        scores = logits_v[...].astype(jnp.float32)
        highest = jnp.max(scores, axis=1, keepdims=True)
        expd = jnp.exp(scores - highest)
        probability = expd * (1.0 / jnp.sum(expd, axis=1, keepdims=True))
        classes = lax.broadcasted_iota(jnp.int32, scores.shape, 1)
        gradient = probability - jnp.where(classes == target, 1.0, 0.0)
        grad[...] = jnp.zeros_like(grad)
        grad[pl.ds(pl.multiple_of(c * rows, rows), rows), :] = gradient.astype(jnp.bfloat16)
        sketch = lax.dot_general(proj_ref[...], grad[...], NT, preferred_element_type=jnp.float32)
        hessian = jnp.sum(probability * (1.0 - probability), axis=1, keepdims=True)
        lane = lax.broadcasted_iota(jnp.int32, (rows, LANES), 1)
        line = lax.broadcasted_iota(jnp.int32, (rows, LANES), 0)
        hessian = jnp.sum(jnp.where(lane == line + (1 - c) * rows, hessian, 0.0), axis=0, keepdims=True)
        leaf = pltpu.roll(leaf_ref[pl.ds(x * NY + y, 1), :].astype(jnp.float32), rows, 1)
        lane = lax.broadcasted_iota(jnp.int32, (K, LANES), 1)
        line = lax.broadcasted_iota(jnp.int32, (K, LANES), 0)
        beside = jnp.where(line == 0, hessian, jnp.where(line == 1, leaf, 0.0))
        rows_s[...] = jnp.where(lane // rows == c, sketch, beside).astype(jnp.bfloat16)

    with jax.named_scope("regroup"):
        fetches[0].wait()
        width = NY * LANES
        for d in range(NZ):
            four = bins_v[d * GROUP : (d + 1) * GROUP, :].astype(jnp.float32)
            bins_s[d] = jnp.concatenate(
                [four[:, i * width : (i + 1) * width] for i in range(NX)], axis=0
            ).astype(jnp.bfloat16)

        src = lax.broadcasted_iota(jnp.int32, (cols, cols), 0)
        dst = lax.broadcasted_iota(jnp.int32, (cols, cols), 1)
        same = (src // BINS) == (dst // BINS)
        steps[0] = jnp.where(same & (src <= dst), 1.0, 0.0).astype(jnp.bfloat16)
        steps[1] = jnp.where(same & (src > dst), 1.0, 0.0).astype(jnp.bfloat16)

    with jax.named_scope("barrier"):
        pl.semaphore_wait(barrier, 2 * NZ - 1 + NY - 1 + NX - 1)

    def to_column(t, src, dst, kind, act):
        device = dev(x, y, (z + far_first(t, NZ)) % NZ, h)
        here = (t == NZ - 1) & (c == h)

        @pl.when(here)
        def _():
            if act == "start":
                pltpu.make_async_copy(src, dst, column_sem.at[kind]).start()

        @pl.when(jnp.logical_not(here))
        def _():
            copy = remote(src, dst, send_sem.at[kind], column_sem.at[kind], device)
            if act == "start":
                copy.start()
            else:
                copy.wait_send()

    def column_values(t, act):
        to_column(t, rows_s, rows_r.at[slot], 0, act)

    def column_bins(t, act):
        to_column(t, bins_s.at[(z + far_first(t, NZ)) % NZ], bins_r.at[slot], 1, act)

    @pl.loop(0, NZ)
    def _(t):
        column_values(t, "start")

    @pl.loop(0, NZ)
    def _(t):
        column_bins(t, "start")

    def await_bytes(ref, sem):
        pltpu.make_async_copy(ref, ref, sem).wait()

    with jax.named_scope("zvalues"):
        await_bytes(rows_r, column_sem.at[0])
        first = lax.broadcasted_iota(jnp.int32, (1, LANES), 1) < rows
        line = lax.broadcasted_iota(jnp.int32, (K, LANES), 0)
        beside = jnp.zeros((K, LANES), jnp.float32)
        for i in range(HZ):
            low, high = rows_r[2 * i].astype(jnp.float32), rows_r[2 * i + 1].astype(jnp.float32)
            vals[x, y, :, i * LANES : (i + 1) * LANES] = jnp.where(first, low, high).astype(jnp.bfloat16)
            other = pltpu.roll(jnp.where(first, high, low), rows, 1)
            beside = jnp.where(line == i, other[0:1], jnp.where(line == HZ + i, other[1:2], beside))
        vals[x, y, :, HZ * LANES :] = beside.astype(jnp.bfloat16)

    def y_copy(t):
        device = dev(x, (y + far_first(t, NY)) % NY, z, c)
        return remote(vals.at[x, y], vals.at[x, y], send_sem.at[2], y_sem.at[y], device)

    def x_copy(t, ys, sem):
        device = dev((x + far_first(t, NX)) % NX, y, z, c)
        return remote(vals.at[x, ys], vals.at[x, ys], send_sem.at[3], sem.at[x], device)

    def near_y(t):
        return (y + near_first(t) + NY) % NY

    def near_x(t):
        return (x + near_first(t) + NX) % NX

    @pl.loop(0, NX - 1)
    def _(t):
        x_copy(t, y, direct_sem).start()

    @pl.loop(0, NY - 1)
    def _(t):
        y_copy(t).start()

    acc[...] = jnp.zeros_like(acc)

    @pl.loop(1, NX)
    def _(i):
        xs = near_x(i)
        await_bytes(vals.at[xs, y], direct_sem.at[xs])

        @pl.loop(1, NEAR + 1)
        def _(t):
            block = vals.at[xs, y]
            remote(block, block, send_sem.at[3], near_sem.at[xs], dev(x, near_y(t), z, c)).start()

    def await_y(t):
        ys = near_y(t)
        await_bytes(vals.at[x, ys], y_sem.at[ys])
        return ys

    @pl.loop(NEAR + 1, NY)
    def _(i):
        ys = await_y(i)

        @pl.loop(0, NX - 1)
        def _(t):
            x_copy(t, ys, far_sem).start()

    @pl.loop(1, NEAR + 1)
    def _(i):
        await_y(i)

    with jax.named_scope("zbins"):
        await_bytes(bins_r, column_sem.at[1])

        @pl.loop(0, 2 * HZ)
        def _(i):
            for j in range(NY):
                bins_f[i, j] = bins_r[i, :, j * LANES : (j + 1) * LANES].astype(jnp.float32)

    bin_ids = lax.broadcasted_iota(jnp.int32, (BINS, LANES), 0).astype(jnp.float32).astype(jnp.bfloat16)
    leaf_ids = lax.broadcasted_iota(jnp.int32, (LEAVES, LANES), 0).astype(jnp.float32).astype(jnp.bfloat16)
    one, nil = jnp.bfloat16(1), jnp.bfloat16(0)

    def add_blocks(xs, start, count):
        for b in range(count):
            ys = near_y(start + b)
            beside = vals[xs, ys, :, HZ * LANES :].astype(jnp.float32)
            for i in range(HZ):
                src = slice(i * LANES, (i + 1) * LANES)
                at = (b * HZ + i) * LANES
                dst = slice(at, at + LANES)
                hess = jnp.broadcast_to(beside[i : i + 1], (LEAVES, LANES)).astype(jnp.bfloat16)
                leaf = jnp.broadcast_to(beside[HZ + i : HZ + i + 1], (LEAVES, LANES)).astype(jnp.bfloat16)
                tile = vals[xs, ys, :, src]
                for l in range(LEAVES):
                    weights[l * K : (l + 1) * K, dst] = jnp.where(leaf == jnp.bfloat16(l), tile, nil)
                weights[LEAVES * K :, dst] = jnp.where(leaf == leaf_ids, hess, nil)
                for side, core in enumerate((1 - c, c)):
                    for f in range(GROUP):
                        ids = bins_f[2 * i + core, ys, pl.ds(xs * GROUP + f, 1), :]
                        ids = jnp.broadcast_to(ids, (BINS, LANES)).astype(jnp.bfloat16)
                        onehot[side, f * BINS : (f + 1) * BINS, dst] = jnp.where(ids == bin_ids, one, nil)
        depth = slice(0, count * HZ * LANES)
        for side in range(2):
            acc[side] += lax.dot_general(
                weights[:, depth], onehot[side, :, depth], NT, preferred_element_type=jnp.float32
            )

    with jax.named_scope("slabs"):

        @pl.loop(0, NY // NEAR)
        def _(t):
            add_blocks(x, t * NEAR, NEAR)

        @pl.loop(1, NX)
        def _(i):
            xs = near_x(i)
            await_bytes(vals.at[xs, pl.ds(0, NEAR)], near_sem.at[xs])
            add_blocks(xs, 0, NEAR + 1)

        @pl.loop(1, NX)
        def _(i):
            xs = near_x(i)
            await_bytes(vals.at[xs, pl.ds(0, NY - 1 - NEAR)], far_sem.at[xs])
            add_blocks(xs, NEAR + 1, NY - 1 - NEAR)

    swap = remote(acc.at[0], hist_r, swap_sem.at[0], swap_sem.at[1], dev(x, y, z, 1 - c))
    swap.start()
    with jax.named_scope("cores"):
        swap.wait_recv()

    with jax.named_scope("gains"):
        hist = acc[1] + hist_r[...]
        left = jnp.zeros_like(hist)
        right = jnp.zeros_like(hist)
        rest = hist
        for _ in range(3):
            piece = rest.astype(jnp.bfloat16)
            rest = rest - piece.astype(jnp.float32)
            left += jnp.dot(piece, steps[0], preferred_element_type=jnp.float32)
            right += jnp.dot(piece, steps[1], preferred_element_type=jnp.float32)
        for i in range(cols // LANES):
            sums[0, i] = left[:, i * LANES : (i + 1) * LANES]
            sums[1, i] = right[:, i * LANES : (i + 1) * LANES]

        def side_sums(side, lines):
            return jnp.concatenate([sums[side, i, lines, :] for i in range(cols // LANES)], axis=1)

        def squares(get):
            total = jnp.zeros((LEAVES, cols), jnp.float32)
            for k in range(K):
                s = get(pl.ds(k, LEAVES, stride=K))
                total += s * s
            return total / (get(slice(LEAVES * K, LEAVES * K + LEAVES)) + ridge)

        gain = (
            squares(lambda r: side_sums(0, r))
            + squares(lambda r: side_sums(1, r))
            - squares(lambda r: side_sums(0, r) + side_sums(1, r))
        )
        lane = lax.broadcasted_iota(jnp.int32, (1, cols), 1)
        counts = jnp.zeros((1, cols), jnp.int32)
        fetches[5].wait()
        for f in range(GROUP):
            counts = jnp.where(lane // BINS == f, nbins_ref[z * GROUP + f], counts)
        gain = jnp.where(lane % BINS < counts - 1, gain, 0.0)
        best = jnp.broadcast_to(jnp.max(gain, axis=1, keepdims=True), (LEAVES, LANES))
        for i in range(NZ):
            gain_s[i] = gain[i * LP : (i + 1) * LP]
            peak_s[i] = best[i * LP : (i + 1) * LP]

    def gain_copy(t):
        other = (z + far_first(t, NZ)) % NZ
        return remote(gain_s.at[other], gain_r.at[z], gain_sem.at[0], gain_sem.at[1], dev(x, y, other, c))

    def peak_copy(t):
        other = (z + far_first(t, NZ)) % NZ
        return remote(peak_s.at[other], peak_r.at[z], peak_sem.at[0], peak_sem.at[1], dev(x, y, other, 1 - c))

    plane = [(i, j) for i in range(NX) for j in range(NY) if i or j]
    plane.sort(key=lambda step: -min(step[0], NX - step[0]) - min(step[1], NY - step[1]))
    here = x * NY + y

    def best_copy(t):
        i, j = plane[t]
        device = dev((x + i) % NX, (y + j) % NY, z, c)
        return remote(best_s, best_r.at[here], best_sem.at[0], best_sem.at[1], device)

    with jax.named_scope("column"):

        @pl.loop(0, NZ - 1)
        def _(t):
            peak_copy(t).start()
            gain_copy(t).start()

        peak_copy(NZ - 1).start()
        gain_r[z] = gain_s[z]

        await_bytes(gain_r.at[pl.ds(0, NZ - 1)], gain_sem.at[1])
        await_bytes(peak_r, peak_sem.at[1])
        best = jnp.max(functools.reduce(jnp.maximum, [gain_r[i] for i in range(NZ)]), axis=1, keepdims=True)
        best_s[...] = functools.reduce(jnp.maximum, [peak_r[i] for i in range(NZ)] + [best])

    with jax.named_scope("plane"):
        for t in range(NX * NY - 1):
            best_copy(t).start()
        best_r[here] = best_s[...]

        @pl.loop(0, NZ)
        def _(t):
            column_values(t, "wait")
            column_bins(t, "wait")

        await_bytes(vals.at[0, pl.ds(0, NY - 1)], send_sem.at[2])
        await_bytes(vals.at[pl.ds(0, NX - 1)], send_sem.at[3])
        swap.wait_send()
        await_bytes(peak_s, peak_sem.at[0])
        await_bytes(gain_s.at[pl.ds(0, NZ - 1)], gain_sem.at[0])

        await_bytes(best_r.at[pl.ds(0, NX * NY - 1)], best_sem.at[1])
        best = functools.reduce(jnp.maximum, [best_r[i] for i in range(NX * NY)])[:, :1]
        for i in range(NZ):
            out_ref[:, i * cols : (i + 1) * cols] = gain_r[i] / (best + epsilon)

        await_bytes(best_r.at[pl.ds(0, NX * NY - 1)], best_sem.at[0])


def on_device(NX, NY, NZ, logits, labels, projection, bins, nbins, leaf):
    bf16, f32 = jnp.bfloat16, jnp.float32
    HZ = NZ // 2
    LP = LEAVES // NZ
    rows, classes = logits.shape
    span = HZ * LANES
    cols = GROUP * BINS
    tall = LEAVES * (K + 1)
    VMEM, DMA = pltpu.VMEM, pltpu.SemaphoreType.DMA
    vmem = pl.BlockSpec(memory_space=pltpu.VMEM)
    hbm = pl.BlockSpec(memory_space=pl.ANY)
    bin_block = (GROUP * NX, NY * LANES)
    return pl.pallas_call(
        functools.partial(kernel, NX, NY, NZ),
        out_shape=jax.ShapeDtypeStruct((LP, NZ * cols), f32),
        in_specs=[hbm] * 6,
        out_specs=vmem,
        scratch_shapes=[
            VMEM(logits.shape, bf16),
            VMEM((1, rows), jnp.int32),
            VMEM((K, classes), bf16),
            VMEM(bins.shape, jnp.int32),
            pltpu.SMEM(nbins.shape, jnp.int32),
            VMEM((NX * NY, LANES), jnp.int32),
            VMEM((2 * rows, classes), bf16),
            VMEM((NZ, *bin_block), bf16),
            VMEM((K, LANES), bf16),
            VMEM((NZ, *bin_block), bf16),
            VMEM((NZ, K, LANES), bf16),
            VMEM((NZ, NY, GROUP * NX, LANES), f32),
            VMEM((NX, NY, K, span + LANES), bf16),
            VMEM((tall, (NY // 2 + 1) * span), bf16),
            VMEM((2, cols, (NY // 2 + 1) * span), bf16),
            VMEM((2, cols, cols), bf16),
            VMEM((2, tall, cols), f32),
            VMEM((tall, cols), f32),
            VMEM((2, cols // LANES, tall, LANES), f32),
            VMEM((NZ, LP, cols), f32),
            VMEM((NZ, LP, cols), f32),
            VMEM((NZ, LP, LANES), f32),
            VMEM((NZ, LP, LANES), f32),
            VMEM((LP, LANES), f32),
            VMEM((NX * NY, LP, LANES), f32),
            DMA((6,)),
            DMA((2,)),
            DMA((4,)),
            DMA((NY,)),
            DMA((NX,)),
            DMA((NX,)),
            DMA((NX,)),
            DMA((2,)),
            DMA((2,)),
            DMA((2,)),
            DMA((2,)),
        ],
        compiler_params=pltpu.CompilerParams(
            collective_id=0, has_side_effects=True, vmem_limit_bytes=62 * 2**20
        ),
        cost_estimate=pl.CostEstimate(
            flops=2 * tall * 2 * cols * NX * NY * span, bytes_accessed=2**20, transcendentals=rows * classes
        ),
    )(
        logits,
        labels.reshape(1, rows),
        projection.T,
        bins,
        nbins,
        leaf.reshape(NX * NY, LANES),
    )


def solution(mesh, NX=4, NY=8):
    return jax.shard_map(
        functools.partial(on_device, NX, NY, mesh.shape["row"]),
        mesh=mesh,
        in_specs=(
            P(("row", "feat"), None),
            P(("row", "feat")),
            P(),
            P("feat", "row"),
            P("feat"),
            P("row"),
        ),
        out_specs=P("row", "feat"),
        check_vma=False,
    )
```

```python
import functools

import jax
import jax.numpy as jnp
from jax import lax
from jax.experimental import pallas as pl
from jax.experimental.pallas import tpu as pltpu
from jax.sharding import PartitionSpec as P

BINS = 64
LEAVES = 16
K = 16
GROUP = 4
LANES = 128
MESH = pl.DeviceIdType.MESH
NT = (((1,), (1,)), ((), ()))

ridge = 1.0
epsilon = 1e-6


def near_first(t):
    return ((t + 1) // 2) * (2 * (t % 2) - 1)


def far_first(t, n):
    return n // 2 + near_first(t)


def kernel(
    NX,
    NY,
    NZ,
    logits_any,
    labels_any,
    proj_any,
    bins_any,
    nbins_any,
    leaf_any,
    out_ref,
    logits_v,
    labels_ref,
    proj_ref,
    bins_v,
    nbins_ref,
    leaf_ref,
    grad,
    bins_s,
    rows_s,
    bins_r,
    rows_r,
    bins_f,
    vals,
    weights,
    onehot,
    steps,
    acc,
    hist_r,
    sums,
    gain_s,
    gain_r,
    peak_s,
    peak_r,
    best_s,
    best_r,
    local_sem,
    column_sem,
    send_sem,
    y_sem,
    direct_sem,
    near_sem,
    far_sem,
    swap_sem,
    gain_sem,
    peak_sem,
    best_sem,
):
    HZ = NZ // 2
    LP = LEAVES // NZ
    NEAR = NY // 2
    cols = GROUP * BINS
    rows = labels_ref.shape[1]
    z = lax.axis_index("row")
    feat = lax.axis_index("feat")
    c = feat % 2
    y = (feat // 2) % NY
    x = feat // (2 * NY)
    h = z // HZ
    slot = (z % HZ) * 2 + c

    def dev(x_, y_, z_, c_):
        return (z_, (x_ * NY + y_) * 2 + c_)

    def remote(src, dst, send, recv, device):
        return pltpu.make_async_remote_copy(
            src_ref=src, dst_ref=dst, send_sem=send, recv_sem=recv, device_id=device, device_id_type=MESH
        )

    operands = (
        (bins_any, bins_v),
        (logits_any, logits_v),
        (labels_any, labels_ref),
        (proj_any, proj_ref),
        (leaf_any, leaf_ref),
        (nbins_any, nbins_ref),
    )
    fetches = [pltpu.make_async_copy(src, dst, local_sem.at[i]) for i, (src, dst) in enumerate(operands)]
    for fetch in fetches:
        fetch.start()

    barrier = pltpu.get_barrier_semaphore()

    def greet(device):
        pl.semaphore_signal(barrier, inc=1, device_id=device, device_id_type=MESH)

    for t in range(max(NX, NY, NZ)):
        if t < NZ:
            other = (z + far_first(t, NZ)) % NZ
            greet(dev(x, y, other, 1 - c))
            if t < NZ - 1:
                greet(dev(x, y, other, c))
        if t < NY - 1:
            greet(dev(x, (y + far_first(t, NY)) % NY, z, c))
        if t < NX - 1:
            greet(dev((x + far_first(t, NX)) % NX, y, z, c))

    with jax.named_scope("softmax"):
        for fetch in fetches[1:5]:
            fetch.wait()
        lane = lax.broadcasted_iota(jnp.int32, (rows, rows), 1)
        line = lax.broadcasted_iota(jnp.int32, (rows, rows), 0)
        spread = jnp.where(lane == line, labels_ref[...].astype(jnp.float32), 0.0)
        target = jnp.sum(spread, axis=1, keepdims=True).astype(jnp.int32)
        scores = logits_v[...].astype(jnp.float32)
        highest = jnp.max(scores, axis=1, keepdims=True)
        expd = jnp.exp(scores - highest)
        probability = expd * (1.0 / jnp.sum(expd, axis=1, keepdims=True))
        classes = lax.broadcasted_iota(jnp.int32, scores.shape, 1)
        gradient = probability - jnp.where(classes == target, 1.0, 0.0)
        grad[...] = jnp.zeros_like(grad)
        grad[pl.ds(pl.multiple_of(c * rows, rows), rows), :] = gradient.astype(jnp.bfloat16)
        sketch = lax.dot_general(proj_ref[...], grad[...], NT, preferred_element_type=jnp.float32)
        hessian = jnp.sum(probability * (1.0 - probability), axis=1, keepdims=True)
        lane = lax.broadcasted_iota(jnp.int32, (rows, LANES), 1)
        line = lax.broadcasted_iota(jnp.int32, (rows, LANES), 0)
        hessian = jnp.sum(jnp.where(lane == line + (1 - c) * rows, hessian, 0.0), axis=0, keepdims=True)
        leaf = pltpu.roll(leaf_ref[pl.ds(x * NY + y, 1), :].astype(jnp.float32), rows, 1)
        lane = lax.broadcasted_iota(jnp.int32, (K, LANES), 1)
        line = lax.broadcasted_iota(jnp.int32, (K, LANES), 0)
        beside = jnp.where(line == 0, hessian, jnp.where(line == 1, leaf, 0.0))
        rows_s[...] = jnp.where(lane // rows == c, sketch, beside).astype(jnp.bfloat16)

    with jax.named_scope("regroup"):
        fetches[0].wait()
        width = NY * LANES
        for d in range(NZ):
            four = bins_v[d * GROUP : (d + 1) * GROUP, :].astype(jnp.float32)
            bins_s[d] = jnp.concatenate(
                [four[:, i * width : (i + 1) * width] for i in range(NX)], axis=0
            ).astype(jnp.bfloat16)

        src = lax.broadcasted_iota(jnp.int32, (cols, cols), 0)
        dst = lax.broadcasted_iota(jnp.int32, (cols, cols), 1)
        same = (src // BINS) == (dst // BINS)
        steps[0] = jnp.where(same & (src <= dst), 1.0, 0.0).astype(jnp.bfloat16)
        steps[1] = jnp.where(same & (src > dst), 1.0, 0.0).astype(jnp.bfloat16)

    with jax.named_scope("barrier"):
        pl.semaphore_wait(barrier, 2 * NZ - 1 + NY - 1 + NX - 1)

    def to_column(t, src, dst, kind, act):
        device = dev(x, y, (z + far_first(t, NZ)) % NZ, h)
        here = (t == NZ - 1) & (c == h)

        @pl.when(here)
        def _():
            if act == "start":
                pltpu.make_async_copy(src, dst, column_sem.at[kind]).start()

        @pl.when(jnp.logical_not(here))
        def _():
            copy = remote(src, dst, send_sem.at[kind], column_sem.at[kind], device)
            if act == "start":
                copy.start()
            else:
                copy.wait_send()

    def column_values(t, act):
        to_column(t, rows_s, rows_r.at[slot], 0, act)

    def column_bins(t, act):
        to_column(t, bins_s.at[(z + far_first(t, NZ)) % NZ], bins_r.at[slot], 1, act)

    @pl.loop(0, NZ)
    def _(t):
        column_values(t, "start")

    @pl.loop(0, NZ)
    def _(t):
        column_bins(t, "start")

    def await_bytes(ref, sem):
        pltpu.make_async_copy(ref, ref, sem).wait()

    with jax.named_scope("zvalues"):
        await_bytes(rows_r, column_sem.at[0])
        first = lax.broadcasted_iota(jnp.int32, (1, LANES), 1) < rows
        line = lax.broadcasted_iota(jnp.int32, (K, LANES), 0)
        beside = jnp.zeros((K, LANES), jnp.float32)
        for i in range(HZ):
            low, high = rows_r[2 * i].astype(jnp.float32), rows_r[2 * i + 1].astype(jnp.float32)
            vals[x, y, :, i * LANES : (i + 1) * LANES] = jnp.where(first, low, high).astype(jnp.bfloat16)
            other = pltpu.roll(jnp.where(first, high, low), rows, 1)
            beside = jnp.where(line == i, other[0:1], jnp.where(line == HZ + i, other[1:2], beside))
        vals[x, y, :, HZ * LANES :] = beside.astype(jnp.bfloat16)

    def y_copy(t):
        device = dev(x, (y + far_first(t, NY)) % NY, z, c)
        return remote(vals.at[x, y], vals.at[x, y], send_sem.at[2], y_sem.at[y], device)

    def x_copy(t, ys, sem):
        device = dev((x + far_first(t, NX)) % NX, y, z, c)
        return remote(vals.at[x, ys], vals.at[x, ys], send_sem.at[3], sem.at[x], device)

    def near_y(t):
        return (y + near_first(t) + NY) % NY

    def near_x(t):
        return (x + near_first(t) + NX) % NX

    @pl.loop(0, NX - 1)
    def _(t):
        x_copy(t, y, direct_sem).start()

    @pl.loop(0, NY - 1)
    def _(t):
        y_copy(t).start()

    acc[...] = jnp.zeros_like(acc)

    @pl.loop(1, NX)
    def _(i):
        xs = near_x(i)
        await_bytes(vals.at[xs, y], direct_sem.at[xs])

        @pl.loop(1, NEAR + 1)
        def _(t):
            block = vals.at[xs, y]
            remote(block, block, send_sem.at[3], near_sem.at[xs], dev(x, near_y(t), z, c)).start()

    def await_y(t):
        ys = near_y(t)
        await_bytes(vals.at[x, ys], y_sem.at[ys])
        return ys

    @pl.loop(NEAR + 1, NY)
    def _(i):
        ys = await_y(i)

        @pl.loop(0, NX - 1)
        def _(t):
            x_copy(t, ys, far_sem).start()

    @pl.loop(1, NEAR + 1)
    def _(i):
        await_y(i)

    with jax.named_scope("zbins"):
        await_bytes(bins_r, column_sem.at[1])

        @pl.loop(0, 2 * HZ)
        def _(i):
            for j in range(NY):
                bins_f[i, j] = bins_r[i, :, j * LANES : (j + 1) * LANES].astype(jnp.float32)

    bin_ids = lax.broadcasted_iota(jnp.int32, (BINS, LANES), 0).astype(jnp.float32).astype(jnp.bfloat16)
    leaf_ids = lax.broadcasted_iota(jnp.int32, (LEAVES, LANES), 0).astype(jnp.float32).astype(jnp.bfloat16)
    one, nil = jnp.bfloat16(1), jnp.bfloat16(0)

    swap = remote(acc.at[0], hist_r, swap_sem.at[0], swap_sem.at[1], dev(x, y, z, 1 - c))

    def add_blocks(xs, start, count, last=False):
        for b in range(count):
            ys = near_y(start + b)
            beside = vals[xs, ys, :, HZ * LANES :].astype(jnp.float32)
            for i in range(HZ):
                src = slice(i * LANES, (i + 1) * LANES)
                at = (b * HZ + i) * LANES
                dst = slice(at, at + LANES)
                hess = jnp.broadcast_to(beside[i : i + 1], (LEAVES, LANES)).astype(jnp.bfloat16)
                leaf = jnp.broadcast_to(beside[HZ + i : HZ + i + 1], (LEAVES, LANES)).astype(jnp.bfloat16)
                tile = vals[xs, ys, :, src]
                for l in range(LEAVES):
                    weights[l * K : (l + 1) * K, dst] = jnp.where(leaf == jnp.bfloat16(l), tile, nil)
                weights[LEAVES * K :, dst] = jnp.where(leaf == leaf_ids, hess, nil)
                for side, core in enumerate((1 - c, c)):
                    for f in range(GROUP):
                        ids = bins_f[2 * i + core, ys, pl.ds(xs * GROUP + f, 1), :]
                        ids = jnp.broadcast_to(ids, (BINS, LANES)).astype(jnp.bfloat16)
                        onehot[side, f * BINS : (f + 1) * BINS, dst] = jnp.where(ids == bin_ids, one, nil)
        depth = slice(0, count * HZ * LANES)
        for side in range(2):
            if side == 1 and last:
                swap.start()
            acc[side] += lax.dot_general(
                weights[:, depth], onehot[side, :, depth], NT, preferred_element_type=jnp.float32
            )

    with jax.named_scope("slabs"):

        @pl.loop(0, NY // NEAR)
        def _(t):
            add_blocks(x, t * NEAR, NEAR)

        @pl.loop(1, NX)
        def _(i):
            xs = near_x(i)
            await_bytes(vals.at[xs, pl.ds(0, NEAR)], near_sem.at[xs])
            add_blocks(xs, 0, NEAR + 1)

        def add_far(i, last=False):
            xs = near_x(i)
            await_bytes(vals.at[xs, pl.ds(0, NY - 1 - NEAR)], far_sem.at[xs])
            add_blocks(xs, NEAR + 1, NY - 1 - NEAR, last)

        pl.loop(1, NX - 1)(add_far)
        add_far(NX - 1, True)

    with jax.named_scope("cores"):
        swap.wait_recv()

    with jax.named_scope("gains"):
        hist = acc[1] + hist_r[...]
        left = jnp.zeros_like(hist)
        right = jnp.zeros_like(hist)
        rest = hist
        for _ in range(3):
            piece = rest.astype(jnp.bfloat16)
            rest = rest - piece.astype(jnp.float32)
            left += jnp.dot(piece, steps[0], preferred_element_type=jnp.float32)
            right += jnp.dot(piece, steps[1], preferred_element_type=jnp.float32)
        for i in range(cols // LANES):
            sums[0, i] = left[:, i * LANES : (i + 1) * LANES]
            sums[1, i] = right[:, i * LANES : (i + 1) * LANES]

        def side_sums(side, lines):
            return jnp.concatenate([sums[side, i, lines, :] for i in range(cols // LANES)], axis=1)

        def squares(get):
            total = jnp.zeros((LEAVES, cols), jnp.float32)
            for k in range(K):
                s = get(pl.ds(k, LEAVES, stride=K))
                total += s * s
            return total / (get(slice(LEAVES * K, LEAVES * K + LEAVES)) + ridge)

        gain = (
            squares(lambda r: side_sums(0, r))
            + squares(lambda r: side_sums(1, r))
            - squares(lambda r: side_sums(0, r) + side_sums(1, r))
        )
        lane = lax.broadcasted_iota(jnp.int32, (1, cols), 1)
        counts = jnp.zeros((1, cols), jnp.int32)
        fetches[5].wait()
        for f in range(GROUP):
            counts = jnp.where(lane // BINS == f, nbins_ref[z * GROUP + f], counts)
        gain = jnp.where(lane % BINS < counts - 1, gain, 0.0)
        best = jnp.broadcast_to(jnp.max(gain, axis=1, keepdims=True), (LEAVES, LANES))
        for i in range(NZ):
            gain_s[i] = gain[i * LP : (i + 1) * LP]
            peak_s[i] = best[i * LP : (i + 1) * LP]

    def gain_copy(t):
        other = (z + far_first(t, NZ)) % NZ
        return remote(gain_s.at[other], gain_r.at[z], gain_sem.at[0], gain_sem.at[1], dev(x, y, other, c))

    def peak_copy(t):
        other = (z + far_first(t, NZ)) % NZ
        return remote(peak_s.at[other], peak_r.at[z], peak_sem.at[0], peak_sem.at[1], dev(x, y, other, 1 - c))

    plane = [(i, j) for i in range(NX) for j in range(NY) if i or j]
    plane.sort(key=lambda step: -min(step[0], NX - step[0]) - min(step[1], NY - step[1]))
    here = x * NY + y

    def best_copy(t):
        i, j = plane[t]
        device = dev((x + i) % NX, (y + j) % NY, z, c)
        return remote(best_s, best_r.at[here], best_sem.at[0], best_sem.at[1], device)

    with jax.named_scope("column"):

        @pl.loop(0, NZ - 1)
        def _(t):
            peak_copy(t).start()
            gain_copy(t).start()

        peak_copy(NZ - 1).start()
        gain_r[z] = gain_s[z]

        await_bytes(gain_r.at[pl.ds(0, NZ - 1)], gain_sem.at[1])
        await_bytes(peak_r, peak_sem.at[1])
        best = jnp.max(functools.reduce(jnp.maximum, [gain_r[i] for i in range(NZ)]), axis=1, keepdims=True)
        best_s[...] = functools.reduce(jnp.maximum, [peak_r[i] for i in range(NZ)] + [best])

    with jax.named_scope("plane"):
        for t in range(NX * NY - 1):
            best_copy(t).start()
        best_r[here] = best_s[...]

        @pl.loop(0, NZ)
        def _(t):
            column_values(t, "wait")
            column_bins(t, "wait")

        await_bytes(vals.at[0, pl.ds(0, NY - 1)], send_sem.at[2])
        await_bytes(vals.at[pl.ds(0, NX - 1)], send_sem.at[3])
        swap.wait_send()
        await_bytes(peak_s, peak_sem.at[0])
        await_bytes(gain_s.at[pl.ds(0, NZ - 1)], gain_sem.at[0])

        await_bytes(best_r.at[pl.ds(0, NX * NY - 1)], best_sem.at[1])
        best = functools.reduce(jnp.maximum, [best_r[i] for i in range(NX * NY)])[:, :1]
        for i in range(NZ):
            out_ref[:, i * cols : (i + 1) * cols] = gain_r[i] / (best + epsilon)

        await_bytes(best_r.at[pl.ds(0, NX * NY - 1)], best_sem.at[0])


def on_device(NX, NY, NZ, logits, labels, projection, bins, nbins, leaf):
    bf16, f32 = jnp.bfloat16, jnp.float32
    HZ = NZ // 2
    LP = LEAVES // NZ
    rows, classes = logits.shape
    span = HZ * LANES
    cols = GROUP * BINS
    tall = LEAVES * (K + 1)
    VMEM, DMA = pltpu.VMEM, pltpu.SemaphoreType.DMA
    vmem = pl.BlockSpec(memory_space=pltpu.VMEM)
    hbm = pl.BlockSpec(memory_space=pl.ANY)
    bin_block = (GROUP * NX, NY * LANES)
    return pl.pallas_call(
        functools.partial(kernel, NX, NY, NZ),
        out_shape=jax.ShapeDtypeStruct((LP, NZ * cols), f32),
        in_specs=[hbm] * 6,
        out_specs=vmem,
        scratch_shapes=[
            VMEM(logits.shape, bf16),
            VMEM((1, rows), jnp.int32),
            VMEM((K, classes), bf16),
            VMEM(bins.shape, jnp.int32),
            pltpu.SMEM(nbins.shape, jnp.int32),
            VMEM((NX * NY, LANES), jnp.int32),
            VMEM((2 * rows, classes), bf16),
            VMEM((NZ, *bin_block), bf16),
            VMEM((K, LANES), bf16),
            VMEM((NZ, *bin_block), bf16),
            VMEM((NZ, K, LANES), bf16),
            VMEM((NZ, NY, GROUP * NX, LANES), f32),
            VMEM((NX, NY, K, span + LANES), bf16),
            VMEM((tall, (NY // 2 + 1) * span), bf16),
            VMEM((2, cols, (NY // 2 + 1) * span), bf16),
            VMEM((2, cols, cols), bf16),
            VMEM((2, tall, cols), f32),
            VMEM((tall, cols), f32),
            VMEM((2, cols // LANES, tall, LANES), f32),
            VMEM((NZ, LP, cols), f32),
            VMEM((NZ, LP, cols), f32),
            VMEM((NZ, LP, LANES), f32),
            VMEM((NZ, LP, LANES), f32),
            VMEM((LP, LANES), f32),
            VMEM((NX * NY, LP, LANES), f32),
            DMA((6,)),
            DMA((2,)),
            DMA((4,)),
            DMA((NY,)),
            DMA((NX,)),
            DMA((NX,)),
            DMA((NX,)),
            DMA((2,)),
            DMA((2,)),
            DMA((2,)),
            DMA((2,)),
        ],
        compiler_params=pltpu.CompilerParams(
            collective_id=0, has_side_effects=True, vmem_limit_bytes=62 * 2**20
        ),
        cost_estimate=pl.CostEstimate(
            flops=2 * tall * 2 * cols * NX * NY * span, bytes_accessed=2**20, transcendentals=rows * classes
        ),
    )(
        logits,
        labels.reshape(1, rows),
        projection.T,
        bins,
        nbins,
        leaf.reshape(NX * NY, LANES),
    )


def solution(mesh, NX=4, NY=8):
    return jax.shard_map(
        functools.partial(on_device, NX, NY, mesh.shape["row"]),
        mesh=mesh,
        in_specs=(
            P(("row", "feat"), None),
            P(("row", "feat")),
            P(),
            P("feat", "row"),
            P("feat"),
            P("row"),
        ),
        out_specs=P("row", "feat"),
        check_vma=False,
    )
```
